256 devices in a mesh: gx: 8 (over z), gy: 4 (over x_lo, core), gz: 8 (over y, x_hi).
Axes of the slice: x: 4 (x_hi: 2, x_lo: 2; x = x_hi * 2 + x_lo), y: 4, z: 8, core: 2. Of those that a mesh axis runs over, the one named last changes fastest.
Arguments:
- recovery_temp: float32 [8192, 128], P(('gx', 'gy', 'gz')), may hold values from 2 to 4
- film_coeff: float32 [8192, 128], P(('gx', 'gy', 'gz')), may hold values from 0.5 to 4
- emissivity: float32 [8192, 128], P(('gx', 'gy', 'gz')), may hold values from 0.6 to 0.95
- char_density: float32 [8192, 128], P(('gx', 'gy', 'gz')), may hold values from 0.5 to 2
- back_temp: float32 [8192, 128], P(('gx', 'gy', 'gz')), may hold values from 0.8 to 1.2
- stencil_frac: float32 [8192, 128], P(('gx', 'gy', 'gz')), may hold values from 0 to 1
- wall_owner: int32 [8192, 1], P(('gx', 'gy', 'gz')), may hold values from 0 to 3; in each aligned block of 32 rows (0 to 31, 32 to 63, ...) at most 16 rows name the same one
- stencil_start: int32 [8192], P(('gx', 'gy', 'gz')), may hold values from 0 to 1023
- live_count: int32 [8192], P(('gx', 'gy', 'gz')), may hold values from 1 to 128
- wall_mask: int32 [256, 128], P('gx', 'gy'), may hold values 0 or 1
- wall_dir: float32 [3, 256, 128], P(None, 'gx', 'gy'), may hold values from -4 to 4
- stiffness: float32 [256, 128, 1024], P('gx', 'gy', 'gz'), may hold values from 0.2 to 5
- start_disp: float32 [3, 256, 128, 1024], P(None, 'gx', 'gy', 'gz'), may hold values from -6 to 6
Outputs:
- surface_temp: float32 [8192, 128], P(('gx', 'gy', 'gz'))
- displacement: float32 [3, 256, 128, 1024], P(None, 'gx', 'gy', 'gz')
The draws below stay inside these ranges and needn't reach their ends.
Inputs may be any that keep to these rules, and one draw needn't show every extreme that they name: `wall_owner`: among the 32 tiles of one device, at most 16 name the same owner, a bound that some block reaches of them.
All inputs are finite; a program needn't handle non-finite values. No bound on the sum of `wall_mask` on one device may be relied on, other than what follows from the above.
Results may differ from the reference program's by a relative error of at most 0.00002.
Values sent between devices are 32-bit elements; how exact they have to be, the bound alone decides.
A program may use at most 256 MiB of HBM per device.

```python
import math
import jax
import jax.numpy as jnp
import numpy as np
from jax import lax

NODES = 128
TILES_DEV = 32
BX = 32
BY = 32
NEWTON = 6
SWEEPS = 4
CAP = 16
OWNERS = 4
TILES = 8192
NX = 256
NY = 128
NZ = 1024
N_GX = 8
N_GY = 4
N_GZ = 8


def set_ends(result, stream_key, least, top_value):
    place = [jax.random.randint(jax.random.fold_in(stream_key, axis), (), 0, length) for axis, length in enumerate(result.shape)]
    widest = result.shape.index(max(result.shape))
    next_to = place[:widest] + [(place[widest] + 1) % result.shape[widest]] + place[widest + 1:]
    return result.at[tuple(place)].set(least).at[tuple(next_to)].set(top_value)


def levels(stream_key, dims, split, low, top_value):
    level = 1.0
    for position, shards_of in split:
        draws = jax.random.uniform(jax.random.fold_in(jax.random.fold_in(stream_key, 6), position), (shards_of,), jnp.float32, low / len(split), top_value / len(split))
        level = level * jnp.repeat(jnp.exp(draws), dims[position] // shards_of).reshape((-1,) + (1,) * (len(dims) - 1 - position))
    return level


def routed_block(own_key, own, number, rows, number_of, top, bound, skew):
    ranking = jax.random.permutation(own_key, number_of)
    heavy_load, common = shares(number_of, rows * top, bound, skew, True), shares(number_of, rows * top, bound, skew, False)
    places = jnp.arange(number_of)

    def named(tallies, turn):
        used = int((tallies > 0).sum())
        fixed = max(1, used // 4)
        shifted = fixed + (places - fixed + turn * (used - fixed)) % max(1, number_of - fixed)
        return jnp.zeros((number_of,), jnp.int32).at[ranking[jnp.where(places < fixed, places, shifted)]].set(jnp.asarray(tallies, jnp.int32))

    tallies = jnp.where(number % 4 == 0, named(heavy_load, number // 4), named(common, number - number // 4 - 1))
    mixed = jax.random.permutation(jax.random.fold_in(own, 3), number_of)
    donor, taker = mixed[0:number_of // 2 * 2:2], mixed[1:number_of // 2 * 2:2]
    slack = jnp.minimum(tallies[donor] - 1, bound - tallies[taker]) // 2
    slack = jnp.where((donor == ranking[0]) | (taker == ranking[0]) | (tallies[taker] == 0), 0, jnp.maximum(slack, 0))
    shifted = jax.random.randint(jax.random.fold_in(own, 4), (number_of // 2,), 0, 1 << 20) % (slack + 1)
    tallies = tallies.at[donor].add(-shifted).at[taker].add(shifted)
    labels = jnp.searchsorted(jnp.cumsum(tallies), jnp.arange(rows * top), side="right").astype(jnp.int32)
    listing = labels.reshape(top, rows).T
    listing = listing[jax.random.permutation(jax.random.fold_in(own, 1), rows)]
    turn = jax.random.randint(jax.random.fold_in(own, 2), (rows, 1), 0, top)
    return jnp.take_along_axis(listing, (jnp.arange(top)[None, :] + turn) % top, axis=1)


def shares(amount, total, limit, skew, full):
    portions = [(1 << 20) // math.isqrt(standing ** skew) + 1 for standing in range(1, amount + 1)]
    largest = limit if full else min(limit, max(-(-total // amount), total * portions[0] // sum(portions)))
    least = 1 if total - largest >= amount - 1 else 0
    given, surplus = [largest] + [least] * (amount - 1), total - largest - least * (amount - 1)
    while surplus > 0:
        free = [i for i in range(1, amount) if given[i] < largest] or [i for i in range(1, amount) if given[i] < limit]
        pool, left = sum([portions[i] for i in free]), surplus
        for i in free:
            extra = min(limit - given[i], max(1, left * portions[i] // pool), surplus)
            given[i] = given[i] + extra
            surplus = surplus - extra
    return np.array(given)


def scatter_about(stream_key, extent, deviation, reach, split=(), kind=jnp.bfloat16):
    level = levels(stream_key, extent, split, -0.22, 0.18) if split else 1.0
    drawn = jax.random.normal(stream_key, extent, jnp.float32) * deviation * level
    return jnp.minimum(jnp.maximum(drawn, -reach), reach).astype(kind)


def setup_inputs(seed: int = 0) -> dict:
    splits = jax.random.split(jax.random.key(seed), 14)
    recovery_temp = jnp.clip(2.0 + 2.0 * jax.random.uniform(splits[0], (TILES, NODES), jnp.float32) ** levels(splits[0], (TILES, NODES), ((0, 256),), -0.2, 0.2), 2.0, 4.0)
    film_coeff = jnp.clip(jnp.exp(math.log(4.0) - 2.0794415 * jax.random.uniform(splits[1], (TILES, NODES), jnp.float32) ** levels(splits[1], (TILES, NODES), ((0, 256),), -0.2, 0.2)), 0.5, 4.0)
    emissivity = jnp.clip(0.6 + 0.34999996 * jax.random.uniform(splits[2], (TILES, NODES), jnp.float32) ** levels(splits[2], (TILES, NODES), ((0, 256),), -0.2, 0.2), 0.6, 0.95)
    char_density = jnp.clip(jnp.exp(math.log(2.0) - 1.3862944 * jax.random.uniform(splits[3], (TILES, NODES), jnp.float32) ** levels(splits[3], (TILES, NODES), ((0, 256),), -0.2, 0.2)), 0.5, 2.0)
    back_temp = jnp.clip(0.8 + 0.40000004 * jax.random.uniform(splits[4], (TILES, NODES), jnp.float32) ** levels(splits[4], (TILES, NODES), ((0, 256),), -0.2, 0.2), 0.8, 1.2)
    stencil_frac = jnp.clip(1.0 * jax.random.uniform(splits[5], (TILES, NODES), jnp.float32) ** levels(splits[5], (TILES, NODES), ((0, 256),), -0.2, 0.2), 0.0, 1.0)
    wall_owner_keys = jax.random.split(jax.random.fold_in(splits[6], 1), TILES // TILES_DEV)
    wall_owner_turns = jax.random.permutation(jax.random.fold_in(splits[6], 3), TILES // TILES_DEV)
    wall_owner = jax.vmap(lambda own, number: routed_block(jax.random.fold_in(splits[6], 2), own, number, TILES_DEV, OWNERS, 1, CAP, 2))(wall_owner_keys, wall_owner_turns).reshape((TILES, 1))
    stencil_start = set_ends(jax.random.randint(splits[7], (TILES,), 0, BX * BY), jax.random.fold_in(splits[7], 1), 0, (BX * BY) - 1).astype(jnp.int32)
    live_count = set_ends(jax.random.randint(splits[8], (TILES,), 1, NODES + 1), jax.random.fold_in(splits[8], 1), 1, NODES).astype(jnp.int32)
    wall_mask = set_ends((jax.random.randint(splits[9], (NX, NY), 0, 4) < 3).astype(jnp.int32), jax.random.fold_in(splits[9], 1), 0, 1)
    wall_dir = scatter_about(splits[10], (3, NX, NY), 1.0, 4.0, ((1, 8), (2, 4)), jnp.float32)
    stiffness = jnp.clip(jnp.exp(math.log(5.0) - 3.218876 * jax.random.uniform(splits[11], (NX, NY, NZ), jnp.float32) ** levels(splits[11], (NX, NY, NZ), ((0, 8), (1, 4), (2, 8)), -0.2, 0.2)), 0.2, 5.0)
    start_disp = scatter_about(splits[12], (3, NX, NY, NZ), 1.0, 6.0, ((1, 8), (2, 4), (3, 8)), jnp.float32)
    return {"recovery_temp": recovery_temp, "film_coeff": film_coeff, "emissivity": emissivity, "char_density": char_density, "back_temp": back_temp, "stencil_frac": stencil_frac, "wall_owner": wall_owner, "stencil_start": stencil_start, "live_count": live_count, "wall_mask": wall_mask, "wall_dir": wall_dir, "stiffness": stiffness, "start_disp": start_disp}


arrhenius_scale = 0.5
activation = 3.0
blowing = 0.5
heat_release = 0.3
radiation = 0.05
conduction = 0.5
time_step = 1.5


def ablation_rate(surface):
    return arrhenius_scale * jnp.exp(activation * (1.0 - 1.0 / surface))


def balance_step(surface, recovery_temp, film_coeff, emissivity, back_temp):
    ablate = ablation_rate(surface)
    factor = 1.0 / (1.0 + blowing * ablate / film_coeff)
    imbalance = (film_coeff * factor * (recovery_temp - surface) + heat_release * ablate
                 - radiation * emissivity * surface ** 4 - conduction * (surface - back_temp))
    slope = film_coeff * factor + 4.0 * radiation * emissivity * surface ** 3 + conduction
    return surface + imbalance / slope


def node_terms(recession, stencil_frac, live_count):
    width = recession.shape[1]
    live = (jnp.arange(width, dtype=jnp.int32)[None, :] < live_count[:, None]).astype(jnp.float32)
    upper = stencil_frac * live
    lower = (1.0 - stencil_frac) * live
    return jnp.stack([lower * recession, upper * recession, lower, upper], axis=1)


def deposit(terms, starts, bases, cells, segments):
    width = terms.shape[2]
    offsets = jnp.arange(width, dtype=jnp.int32)[None, :]
    first = (bases[:, None] + (starts[:, None] + offsets) % cells).reshape(-1)
    second = (bases[:, None] + (starts[:, None] + offsets + 1) % cells).reshape(-1)
    numer = (jax.ops.segment_sum(terms[:, 0].reshape(-1), first, num_segments=segments)
             + jax.ops.segment_sum(terms[:, 1].reshape(-1), second, num_segments=segments))
    denom = (jax.ops.segment_sum(terms[:, 2].reshape(-1), first, num_segments=segments)
             + jax.ops.segment_sum(terms[:, 3].reshape(-1), second, num_segments=segments))
    return numer, denom


def relax(padded, padded_k):
    center_k = padded_k[1:-1, 1:-1, 1:-1]
    inner = slice(1, -1)
    shifts = [(slice(2, None), inner, inner), (slice(None, -2), inner, inner),
              (inner, slice(2, None), inner), (inner, slice(None, -2), inner),
              (inner, inner, slice(2, None)), (inner, inner, slice(None, -2))]
    total = None
    weight = None
    for picked in shifts:
        spring = 0.5 * (center_k + padded_k[picked])
        value = padded[..., picked[0], picked[1], picked[2]]
        if total is None:
            total = spring * value
            weight = spring
        else:
            total = total + spring * value
            weight = weight + spring
    return total / weight


def reference(recovery_temp, film_coeff, emissivity, char_density, back_temp, stencil_frac,
              wall_owner, stencil_start, live_count, wall_mask, wall_dir, stiffness, start_disp):
    surface = back_temp
    for iteration in range(NEWTON):
        surface = balance_step(surface, recovery_temp, film_coeff, emissivity, back_temp)
    recession = time_step * ablation_rate(surface) / char_density
    terms = node_terms(recession, stencil_frac, live_count)
    tiles = recovery_temp.shape[0]
    slab = jnp.arange(tiles, dtype=jnp.int32) // (TILES_DEV * N_GY * N_GZ)
    cells = BX * BY
    bases = (slab * N_GY + wall_owner[:, 0]) * cells
    numer, denom = deposit(terms, stencil_start, bases, cells, N_GX * N_GY * cells)
    face = (numer / (1.0 + denom)).reshape(N_GX, N_GY, BX, BY).transpose(0, 2, 1, 3)
    face = face.reshape(N_GX * BX, N_GY * BY)
    ghost = -wall_mask.astype(jnp.float32) * face * wall_dir
    padded_k = jnp.pad(stiffness, 1)

    def smooth(pair):
        field, plane = pair
        for sweep in range(SWEEPS):
            padded = jnp.pad(field, 1)
            padded = padded.at[1:-1, 1:-1, 0].set(plane)
            field = relax(padded, padded_k)
        return field

    displacement = lax.map(smooth, (start_disp, ghost))
    return surface, displacement
```

```python
import jax
import jax.numpy as jnp
from jax import lax
from jax.experimental import pallas as pl
from jax.experimental.pallas import tpu as pltpu
from jax.sharding import PartitionSpec as P

NEWTON = 6
SWEEPS = 4
MESH = pl.DeviceIdType.MESH
F32 = jnp.float32
SIZES = {"gx": 8, "gy": 4, "gz": 8}
BX = 32
EXT = 40
FLAT = 48 * 128

arrhenius_scale = 0.5
activation = 3.0
blowing = 0.5
heat_release = 0.3
radiation = 0.05
conduction = 0.5
time_step = 1.5


def ablation_rate(surface):
    return arrhenius_scale * jnp.exp(activation * (1.0 - 1.0 / surface))


def balance_step(surface, recovery_temp, film_coeff, emissivity, back_temp):
    ablate = ablation_rate(surface)
    film = film_coeff * film_coeff / (film_coeff + blowing * ablate)
    cubed = surface * surface * surface
    imbalance = (
        film * (recovery_temp - surface)
        + heat_release * ablate
        - radiation * emissivity * (cubed * surface)
        - conduction * (surface - back_temp)
    )
    slope = film + 4.0 * radiation * emissivity * cubed + conduction
    return surface + imbalance / slope


def lanes(shape):
    return lax.broadcasted_iota(jnp.int32, shape, len(shape) - 1)


def rows(shape):
    return lax.broadcasted_iota(jnp.int32, shape, len(shape) - 2)


def place(x):
    start = (x + 16) * 136 + 4
    return start // 128 - 10, start % 128


def kernel(
    recovery_temp, film_coeff, emissivity, char_density, back_temp, stencil_frac,
    wall_owner, stencil_start, live_count, wall_mask, wall_dir, stiffness, start_disp,
    surface_out, disp_out,
    own, below, above, strip_up, strip_down, strip_from_below, strip_from_above,
    slab_up, slab_down, slab_below, slab_above, edge_send, edge_recv,
    slabs, cross_send, cross_recv,
    field_a, field_b, weights, result, thin_weights, thin, source,
    dep_send, dep_recv, ghost, ghost_side, ghost_face, ghost_corner, ghost_all,
    local_sem, send_sem, recv_sem, dep_sem,
):
    gx, gy, gz = (lax.axis_index(a) for a in ("gx", "gy", "gz"))
    position = (gx, gy, gz)
    limits = (SIZES["gx"], SIZES["gy"], SIZES["gz"])

    def there(step):
        found = None
        for p, d, n in zip(position, step, limits):
            if d != 0:
                ok = (p + d >= 0) & (p + d < n)
                found = ok if found is None else found & ok
        return found

    def target(step):
        return tuple(p + d for p, d in zip(position, step))

    def back(step):
        return tuple(-d for d in step)

    on_wall = gz == 0

    class Message:
        def __init__(self, channel, step, src, dst, walls=False):
            self.to, self.origin = there(step), there(back(step))
            if walls:
                self.to, self.origin = self.to & on_wall, self.origin & on_wall
            self.copy = pltpu.make_async_remote_copy(
                src_ref=src, dst_ref=dst, send_sem=send_sem.at[channel], recv_sem=recv_sem.at[channel],
                device_id=target(step), device_id_type=MESH,
            )

        def start(self):
            pl.when(self.to)(self.copy.start)

        def wait_recv(self):
            pl.when(self.origin)(self.copy.wait_recv)

        def wait_send(self):
            pl.when(self.to)(self.copy.wait_send)

    load_u = pltpu.make_async_copy(start_disp, own.at[0:3, :, 0:32], local_sem.at[0])
    load_k = pltpu.make_async_copy(stiffness, own.at[3, :, 0:32], local_sem.at[1])
    load_u.start()
    load_k.start()

    barrier = pltpu.get_barrier_semaphore()
    near = [(1, 0, 0), (-1, 0, 0), (0, 1, 0), (0, -1, 0), (0, 0, 1), (0, 0, -1)]
    near += [(0, a, b) for a in (1, -1) for b in (1, -1)]
    corners = [(a, b, 0) for a in (1, -1) for b in (1, -1)]
    expected = jnp.where(on_wall, 3, 4)

    def greet(step, ok):
        pl.when(ok)(lambda: pl.semaphore_signal(barrier, inc=1, device_id=target(step), device_id_type=MESH))
        return ok.astype(jnp.int32)

    for step in near:
        expected = expected + greet(step, there(step))
    for step in corners:
        expected = expected + greet(step, there(step) & on_wall)
    rank = gy * limits[2] + gz
    for y in range(limits[1]):
        for z in range(limits[2]):
            pl.when(on_wall & (rank != y * limits[2] + z))(
                lambda y=y, z=z: pl.semaphore_signal(barrier, inc=1, device_id=(gx, y, z), device_id_type=MESH)
            )

    back_t = back_temp[...]
    surface = back_t
    for _ in range(NEWTON):
        surface = balance_step(surface, recovery_temp[...], film_coeff[...], emissivity[...], back_t)
    surface_out[...] = surface
    recession = time_step * ablation_rate(surface) / char_density[...]
    shape = (32, 128)
    lane = lanes(shape)
    square = (32, 32)
    diagonal = rows(square) == lanes(square)

    def column(row):
        spread = jnp.broadcast_to(row.astype(F32), square)
        return jnp.broadcast_to(jnp.sum(jnp.where(diagonal, spread, 0.0), axis=1, keepdims=True), shape)

    starts = stencil_start[...]
    shift = column(starts & 127)
    live = lane.astype(F32) < column(live_count[...])
    upper = jnp.where(live, stencil_frac[...], 0.0)
    lower = jnp.where(live, 1.0 - stencil_frac[...], 0.0)
    shift = shift.astype(jnp.int32)
    first, second = [], []
    for low, high in ((lower * recession, upper * recession), (lower, upper)):
        moved = pltpu.roll(high, 1, axis=1)
        spread = low + jnp.where(lane >= 1, moved, 0.0)
        last = jnp.broadcast_to(moved[:, 0:1], shape)
        for bit in range(7):
            spread = jnp.where(((shift >> bit) & 1) == 1, pltpu.roll(spread, 1 << bit, axis=1), spread)
        first.append(jnp.where(lane >= shift, spread, 0.0))
        second.append(jnp.where(lane < shift, spread, jnp.where(lane == shift, last, 0.0)))
    face_row = wall_owner[...] * 8
    row_a = jnp.broadcast_to(face_row + (starts >> 7), square)
    row_b = jnp.broadcast_to(face_row + (((starts >> 7) + 1) & 7), square)

    def gathered(row, terms):
        pick = (rows(square) == row).astype(F32)
        return jnp.dot(pick, terms, precision=lax.Precision.HIGHEST, preferred_element_type=F32)

    summed = gathered(row_a, jnp.concatenate(first, axis=1)) + gathered(row_b, jnp.concatenate(second, axis=1))
    for o in range(4):
        dep_send[o, 0:8] = summed[8 * o : 8 * o + 8, 0:128]
        dep_send[o, 8:16] = summed[8 * o : 8 * o + 8, 128:256]

    tile = (8, 128)
    top = rows(tile) < 4
    load_u.wait()
    load_k.wait()
    group = lanes(shape) // 8
    inner = lanes(shape) % 8 < 4

    def pack_z(c, _):
        halves = []
        for p in range(2):
            packed = jnp.zeros(shape, F32)
            for i in range(16):
                turned = pltpu.roll(own[c, 16 * p + i, 0:32], 8 * i + 4, axis=1)
                packed = jnp.where(group == i, turned, packed)
            halves.append(packed)
        slab_up[c] = jnp.where(inner, halves[0], pltpu.roll(halves[1], 4, axis=1))
        slab_down[c] = jnp.where(inner, pltpu.roll(halves[0], 124, axis=1), halves[1])
        return 0

    lax.fori_loop(0, 4, pack_z, 0)

    def rows_down(a, b):
        return jnp.where(top, a, pltpu.roll(b, 4, axis=0))

    def rows_up(a, b):
        return jnp.where(top, pltpu.roll(b, 4, axis=0), a)

    def pack_y(x, _):
        for pair in range(2):
            a, b = 2 * pair, 2 * pair + 1
            strip_down[pair, x] = rows_down(own[a, x, 0:8], own[b, x, 0:8])
            strip_up[pair, x] = rows_up(own[a, x, 24:32], own[b, x, 24:32])
        return 0

    lax.fori_loop(0, 32, pack_y, 0)
    for pair in range(2):
        a, b = 2 * pair, 2 * pair + 1
        edge_send[0, pair] = rows_down(slab_up[a, 0:8], slab_up[b, 0:8])
        edge_send[1, pair] = rows_up(slab_up[a, 24:32], slab_up[b, 24:32])
        edge_send[2, pair] = rows_down(slab_down[a, 0:8], slab_down[b, 0:8])
        edge_send[3, pair] = rows_up(slab_down[a, 24:32], slab_down[b, 24:32])

    east, west, north, south = (1, 0, 0), (-1, 0, 0), (0, 1, 0), (0, -1, 0)
    x_far = [
        Message(0, east, start_disp.at[:, 28:32], below.at[0:3, :, 0:32]),
        Message(1, east, stiffness.at[28:32], below.at[3, :, 0:32]),
        Message(2, west, start_disp.at[:, 0:4], above.at[0:3, :, 0:32]),
        Message(3, west, stiffness.at[0:4], above.at[3, :, 0:32]),
    ]
    y_far = [Message(4, north, strip_up, strip_from_below), Message(5, south, strip_down, strip_from_above)]
    z_far = [
        Message(6, (0, 0, 1), slab_up, slab_below.at[:, 0:32]),
        Message(7, (0, 0, -1), slab_down, slab_above.at[:, 0:32]),
    ]
    edges = [
        Message(8, (0, -1, 1), edge_send.at[0], edge_recv.at[0]),
        Message(9, (0, 1, 1), edge_send.at[1], edge_recv.at[1]),
        Message(10, (0, -1, -1), edge_send.at[2], edge_recv.at[2]),
        Message(11, (0, 1, -1), edge_send.at[3], edge_recv.at[3]),
    ]

    pl.semaphore_wait(barrier, expected)

    def deposit_copy(y):
        ahead = lax.rem(rank - y * limits[2] + 32, 32)
        slot = jnp.maximum(ahead - 1, 0)
        copy = pltpu.make_async_remote_copy(
            src_ref=dep_send.at[y], dst_ref=dep_recv.at[slot], send_sem=send_sem.at[24 + y], recv_sem=dep_sem.at[0],
            device_id=(gx, y, 0), device_id_type=MESH,
        )
        return ahead != 0, copy

    for message in z_far + edges + y_far:
        message.start()
    for y in range(4):
        away, copy = deposit_copy(y)
        pl.when(away)(copy.start)
    for message in x_far:
        message.start()

    def clear(step, *refs):
        @pl.when(jnp.logical_not(there(step)))
        def _():
            for ref in refs:
                ref[...] = jnp.zeros(ref.shape, F32)

    clear(north, strip_from_above)
    clear(south, strip_from_below)
    clear((0, 0, -1), slab_below.at[:, 0:32])
    clear((0, 0, 1), slab_above.at[:, 0:32])
    for k, message_step in enumerate(((0, -1, 1), (0, 1, 1), (0, -1, -1), (0, 1, -1))):
        clear(back(message_step), edge_recv.at[k])
    clear(west, below.at[:, :, 0:32], below.at[:, 1:4, 32:40], cross_recv.at[0])
    clear(east, above.at[:, :, 0:32], above.at[:, 0:3, 32:40], cross_recv.at[1])
    below[:, 0, 32:40] = jnp.zeros((4, 8, 128), F32)
    above[:, 3, 32:40] = jnp.zeros((4, 8, 128), F32)

    for message in z_far + edges + y_far:
        message.wait_recv()

    def merged(from_above, from_below):
        a = jnp.where(top, from_above, from_below)
        b = pltpu.roll(jnp.where(top, from_below, from_above), 4, axis=0)
        return a, b

    def merge_y(x, _):
        for pair in range(2):
            a, b = merged(strip_from_above[pair, x], strip_from_below[pair, x])
            own[2 * pair, x, 32:40] = a
            own[2 * pair + 1, x, 32:40] = b
        return 0

    lax.fori_loop(0, 32, merge_y, 0)
    for pair in range(2):
        a, b = merged(edge_recv[0, pair], edge_recv[1, pair])
        slab_below[2 * pair, 32:40] = a
        slab_below[2 * pair + 1, 32:40] = b
        a, b = merged(edge_recv[2, pair], edge_recv[3, pair])
        slab_above[2 * pair, 32:40] = a
        slab_above[2 * pair + 1, 32:40] = b
    tall = (EXT, 128)
    tall_inner = lanes(tall) % 8 < 4
    block = lanes(tall) // 32
    up, down = jnp.zeros(tall, F32), jnp.zeros(tall, F32)
    for c in range(4):
        under, over = slab_below[c], slab_above[c]
        left = jnp.where(tall_inner, under, pltpu.roll(over, 4, axis=1))
        right = jnp.where(tall_inner, pltpu.roll(under, 124, axis=1), over)
        slabs[c, 0] = left
        slabs[c, 1] = right
        down = jnp.where(block == c, pltpu.roll(left, 32 * c, axis=1), down)
        up = jnp.where(block == c, pltpu.roll(right, (32 * c + 32) % 128, axis=1), up)
    cross_send[0] = up
    cross_send[1] = down
    x_near = [
        Message(12, east, own.at[:, 29:32, 32:40], below.at[:, 1:4, 32:40]),
        Message(13, west, own.at[:, 0:3, 32:40], above.at[:, 0:3, 32:40]),
        Message(14, east, cross_send.at[0], cross_recv.at[0]),
        Message(15, west, cross_send.at[1], cross_recv.at[1]),
    ]
    for message in x_near:
        message.start()

    @pl.when(on_wall)
    def _():
        everyone = pltpu.make_async_remote_copy(
            src_ref=dep_recv, dst_ref=dep_recv, send_sem=send_sem.at[24], recv_sem=dep_sem.at[0],
            device_id=(gx, 0, 0), device_id_type=MESH,
        )
        everyone.wait_recv()
        total = dep_send[gy]
        for k in range(31):
            total = total + dep_recv[k]
        face = total[0:8] / (1.0 + total[8:16])
        wide = (8, 256)
        acc = jnp.zeros((96, 256), F32)
        for q in range(4):
            mask = wall_mask[pl.ds(q, 8, stride=4), :].astype(F32)
            part = face[:, 32 * q : 32 * q + 32] * (-mask)
            values = jnp.concatenate([part * wall_dir[c, pl.ds(q, 8, stride=4), :] for c in range(3)], axis=1)
            pick = (lanes(wide) == 32 * rows(wide) + 8 * q + 3).astype(F32)
            acc = acc + lax.dot_general(
                values, pick, (((0,), (0,)), ((), ())), precision=lax.Precision.HIGHEST, preferred_element_type=F32
            )
        for c in range(3):
            for p in range(2):
                ghost[p, c] = acc[32 * c : 32 * c + 32, 128 * p : 128 * p + 128]

    g_side = [
        Message(16, north, ghost.at[:, :, 24:32], ghost_side.at[0], True),
        Message(17, south, ghost.at[:, :, 0:8], ghost_side.at[1], True),
    ]
    g_face = [
        Message(18, east, ghost.at[1], ghost_face.at[0], True),
        Message(19, west, ghost.at[0], ghost_face.at[1], True),
    ]
    g_corner = [
        Message(20, (1, 1, 0), ghost.at[1, :, 24:32], ghost_corner.at[0], True),
        Message(21, (1, -1, 0), ghost.at[1, :, 0:8], ghost_corner.at[1], True),
        Message(22, (-1, 1, 0), ghost.at[0, :, 24:32], ghost_corner.at[2], True),
        Message(23, (-1, -1, 0), ghost.at[0, :, 0:8], ghost_corner.at[3], True),
    ]
    g_all = g_side + g_face + g_corner
    for message in g_all:
        message.start()
    clear(south, ghost_side.at[0])
    clear(north, ghost_side.at[1])
    clear(west, ghost_face.at[0])
    clear(east, ghost_face.at[1])
    for k, step in enumerate(((1, 1, 0), (1, -1, 0), (-1, 1, 0), (-1, -1, 0))):
        clear(back(step), ghost_corner.at[k])

    for message in x_far + x_near:
        message.wait_recv()
    for c in range(4):
        low = pltpu.roll(cross_recv[0], (96 - 32 * c) % 128, axis=1)
        high = pltpu.roll(cross_recv[1], (128 - 32 * c) % 128, axis=1)
        slabs[c, 2] = jnp.where(block < 2, high, low)
    tile_lane = lanes(tile)

    def flatten(step, _):
        c, j = lax.div(step, 5), lax.rem(step, 5)

        def put(p, value):
            field_a[c, j, :, 128 * p : 128 * p + 128] = value

        def turned(ref, e, i):
            return pltpu.roll(ref[c, e, pl.ds(j, 8, stride=5), :], 8 * i + 4, axis=1)

        for p in (0, 1, 46, 47):
            put(p, jnp.zeros(tile, F32))
        for first_x, count, ref, base, s in ((-4, 4, below, -4, 2), (0, 16, own, 0, 0), (16, 16, own, 0, 1), (32, 4, above, 32, 2)):
            slab = slabs[c, s, pl.ds(j, 8, stride=5), :]
            before = None
            for x in range(first_x, first_x + count):
                p, at = place(x)
                now = turned(ref, x - base, x % 16)
                value = jnp.where(tile_lane < at, slab, now)
                if before is not None:
                    value = jnp.where(tile_lane < at - 8, before, value)
                put(p, value)
                before = now
            put(p + 1, jnp.where(tile_lane < at, before, slab))
        return 0

    lax.fori_loop(0, 20, flatten, 0)

    N = 4
    ends = tile_lane < 1, tile_lane > 126, tile_lane < 8, tile_lane >= 120

    def column_at(q):
        return pl.ds(pl.multiple_of(q * 128, 128), 128)

    def window(field, c, j, q):
        at = {k: field[c, j, :, column_at(q + k)] for k in range(-2, N + 2)}
        z_up = [pltpu.roll(at[k], 127, axis=1) for k in range(0, N + 1)]
        z_down = [pltpu.roll(at[k], 1, axis=1) for k in range(-1, N)]
        x_up = [pltpu.roll(at[k], 120, axis=1) for k in range(1, N + 2)]
        x_down = [pltpu.roll(at[k], 8, axis=1) for k in range(-2, N - 1)]
        return [
            (
                at[k],
                jnp.where(ends[3], x_up[k + 1], x_up[k]),
                jnp.where(ends[2], x_down[k], x_down[k + 1]),
                jnp.where(ends[1], z_up[k + 1], z_up[k]),
                jnp.where(ends[0], z_down[k], z_down[k + 1]),
            )
            for k in range(N)
        ]

    def part(field, c, j, q):
        if j == 5:
            return pltpu.roll(field[c, 0, :, column_at(q)], 7, axis=0)
        if j == -1:
            return pltpu.roll(field[c, 4, :, column_at(q)], 1, axis=0)
        return field[c, j, :, column_at(q)]

    def weigh(step, _):
        q = 2 + step * N
        for j in range(5):
            for k, (centre, xp, xm, zp, zm) in enumerate(window(field_a, 3, j, q)):
                sides = (xp, xm, part(field_a, 3, j + 1, q + k), part(field_a, 3, j - 1, q + k), zp, zm)
                weight = 6.0 * centre
                for side in sides:
                    weight = weight + side
                inverse = jnp.where(centre > 0.0, 1.0 / weight, 0.0)
                for n, side in enumerate(sides):
                    weights[n, j, :, column_at(q + k)] = (centre + side) * inverse
        return 0

    lax.fori_loop(0, 44 // N, weigh, 0)

    for c in range(3):
        for j in range(5):
            field_b[c, j, :, 0:384] = jnp.zeros((8, 384), F32)
            field_b[c, j, :, 5760:6144] = jnp.zeros((8, 384), F32)
    for sweep, (start, end) in enumerate(((2, 46), (4, 44), (5, 43), (7, 41))):
        src, dst = (field_a, field_b) if sweep % 2 == 0 else (field_b, field_a)

        def relax(step, _, src=src, dst=dst, start=start):
            q = start + step * N
            for j in range(5):
                around = [window(src, c, j, q) for c in range(3)]
                for k in range(N):
                    w = [weights[n, j, :, column_at(q + k)] for n in range(6)]
                    for c in range(3):
                        _, xp, xm, zp, zm = around[c][k]
                        total = w[0] * xp + w[1] * xm
                        total = total + (w[2] * part(src, c, j + 1, q + k) + w[3] * part(src, c, j - 1, q + k))
                        dst[c, j, :, column_at(q + k)] = total + (w[4] * zp + w[5] * zm)
            return 0

        lax.fori_loop(0, -(-(end - start) // N), relax, 0)

    thin[...] = jnp.zeros(thin.shape, F32)

    @pl.when(on_wall)
    def _():
        for message in g_all:
            message.wait_recv()
        for c in range(3):
            for p in range(2):
                ghost_all[c, p, 0:32] = ghost[p, c]
                ghost_all[c, p, 32:40] = jnp.where(top, ghost_side[1, p, c], ghost_side[0, p, c])
            ghost_all[c, 2, 0:32] = jnp.where(lane < 64, ghost_face[1, c], ghost_face[0, c])
            left = tile_lane < 64
            over = jnp.where(left, ghost_corner[3, c], ghost_corner[1, c])
            under = jnp.where(left, ghost_corner[2, c], ghost_corner[0, c])
            ghost_all[c, 2, 32:40] = jnp.where(top, over, under)
        main = tile_lane % 8 >= 4
        octet = tile_lane // 8

        def gather(step, _):
            n, j = lax.div(step, 5), lax.rem(step, 5)
            for s, xs in ((0, range(16)), (1, range(16, 32)), (2, (-4, -3, -2, -1, 32, 33, 34, 35))):
                value = jnp.zeros(tile, F32)
                for x in xs:
                    p, _ = place(x)
                    value = jnp.where(main & (octet == x % 16), weights[n, j, :, 128 * p : 128 * p + 128], value)
                thin_weights[n, j, :, 128 * s : 128 * s + 128] = value
            return 0

        lax.fori_loop(0, 30, gather, 0)
        span = (8, 384)
        for c in range(3):
            for j in range(5):
                wall = jnp.concatenate([ghost_all[c, s, pl.ds(j, 8, stride=5), :] for s in range(3)], axis=1)
                value = thin_weights[5, j] * pltpu.roll(wall, 1, axis=1)
                source[c, j] = value
                thin[0, c, j] = value
        for sweep in range(SWEEPS - 1):
            src, dst = sweep % 2, (sweep + 1) % 2

            def step_thin(c, _, src=src, dst=dst):
                for j in range(5):
                    here = thin[src, c, j]
                    after = thin[src, c, j + 1] if j < 4 else pltpu.roll(thin[src, c, 0], 7, axis=0)
                    prior = thin[src, c, j - 1] if j > 0 else pltpu.roll(thin[src, c, 4], 1, axis=0)
                    total = source[c, j] + thin_weights[0, j] * pltpu.roll(here, 384 - 8, axis=1)
                    total = total + thin_weights[1, j] * pltpu.roll(here, 8, axis=1)
                    total = total + thin_weights[2, j] * after + thin_weights[3, j] * prior
                    total = total + thin_weights[4, j] * pltpu.roll(here, 383, axis=1)
                    thin[dst, c, j] = total + thin_weights[5, j] * pltpu.roll(here, 1, axis=1)
                return 0

            lax.fori_loop(0, 3, step_thin, 0)

    thin_final = (SWEEPS - 1) % 2
    outs = []
    for c in range(3):

        def unflatten(j, _, c=c):
            for s in range(2):
                extra = thin[thin_final, c, j, :, 128 * s : 128 * s + 128]
                for x in range(16 * s, 16 * s + 16):
                    p, at = place(x)
                    low = field_a[c, j, :, 128 * p : 128 * p + 128]
                    low = low + jnp.where(tile_lane < at + 4, extra, 0.0)
                    high = field_a[c, j, :, 128 * p + 128 : 128 * p + 256]
                    value = pltpu.roll(jnp.where(tile_lane >= at, low, high), 128 - at, axis=1)
                    result[c, x, pl.ds(j, 8, stride=5), :] = value
            return 0

        lax.fori_loop(0, 5, unflatten, 0)
        copy = pltpu.make_async_copy(result.at[c, :, 0:32], disp_out.at[c], local_sem.at[2 + c])
        copy.start()
        outs.append(copy)

    for message in x_far + y_far + z_far + edges + x_near + g_all:
        message.wait_send()
    for y in range(4):
        away, copy = deposit_copy(y)
        pl.when(away)(copy.wait_send)
    for copy in outs:
        copy.wait()


def local(
    recovery_temp, film_coeff, emissivity, char_density, back_temp, stencil_frac,
    wall_owner, stencil_start, live_count, wall_mask, wall_dir, stiffness, start_disp,
):
    vmem = pl.BlockSpec(memory_space=pltpu.VMEM)
    hbm = pl.BlockSpec(memory_space=pltpu.HBM)
    scratch = [
        (4, 32, EXT, 128),
        (4, 4, EXT, 128),
        (4, 4, EXT, 128),
        (2, 32, 8, 128),
        (2, 32, 8, 128),
        (2, 32, 8, 128),
        (2, 32, 8, 128),
        (4, 32, 128),
        (4, 32, 128),
        (4, EXT, 128),
        (4, EXT, 128),
        (4, 2, 8, 128),
        (4, 2, 8, 128),
        (4, 3, EXT, 128),
        (2, EXT, 128),
        (2, EXT, 128),
        (4, 5, 8, FLAT),
        (3, 5, 8, FLAT),
        (6, 5, 8, FLAT),
        (3, 32, EXT, 128),
        (6, 5, 8, 384),
        (2, 3, 5, 8, 384),
        (3, 5, 8, 384),
        (4, 16, 128),
        (31, 16, 128),
        (2, 3, 32, 128),
        (2, 2, 3, 8, 128),
        (2, 3, 32, 128),
        (4, 3, 8, 128),
        (3, 3, EXT, 128),
    ]
    return pl.pallas_call(
        kernel,
        out_shape=(
            jax.ShapeDtypeStruct(back_temp.shape, F32),
            jax.ShapeDtypeStruct(start_disp.shape, F32),
        ),
        in_specs=[vmem] * 11 + [hbm] * 2,
        out_specs=(vmem, hbm),
        scratch_shapes=[pltpu.VMEM(s, F32) for s in scratch]
        + [
            pltpu.SemaphoreType.DMA((5,)),
            pltpu.SemaphoreType.DMA((28,)),
            pltpu.SemaphoreType.DMA((24,)),
            pltpu.SemaphoreType.DMA((1,)),
        ],
        compiler_params=pltpu.CompilerParams(collective_id=0, has_side_effects=True, vmem_limit_bytes=60 << 20),
    )(
        recovery_temp, film_coeff, emissivity, char_density, back_temp, stencil_frac,
        wall_owner.reshape(1, 32), stencil_start.reshape(1, 32), live_count.reshape(1, 32),
        wall_mask, wall_dir, stiffness, start_disp,
    )


def solution(mesh):
    tiles = P(("gx", "gy", "gz"), None)
    flat = P(("gx", "gy", "gz"))
    in_specs = (tiles,) * 7 + (flat, flat, P("gx", "gy"), P(None, "gx", "gy"), P("gx", "gy", "gz"), P(None, "gx", "gy", "gz"))
    out_specs = (tiles, P(None, "gx", "gy", "gz"))
    return jax.shard_map(local, mesh=mesh, in_specs=in_specs, out_specs=out_specs, check_vma=False)
```

```python
import jax
import jax.numpy as jnp
from jax import lax
from jax.experimental import pallas as pl
from jax.experimental.pallas import tpu as pltpu
from jax.sharding import PartitionSpec as P

NEWTON = 6
SWEEPS = 4
MESH = pl.DeviceIdType.MESH
F32 = jnp.float32
SIZES = {"gx": 8, "gy": 4, "gz": 8}
EXT = 40

arrhenius_scale = 0.5
activation = 3.0
blowing = 0.5
heat_release = 0.3
radiation = 0.05
conduction = 0.5
time_step = 1.5


def ablation_rate(surface):
    return arrhenius_scale * jnp.exp(activation * (1.0 - 1.0 / surface))


def balance_step(surface, recovery_temp, film_coeff, emissivity, back_temp):
    ablate = ablation_rate(surface)
    film = film_coeff * film_coeff / (film_coeff + blowing * ablate)
    cubed = surface * surface * surface
    imbalance = (
        film * (recovery_temp - surface)
        + heat_release * ablate
        - radiation * emissivity * (cubed * surface)
        - conduction * (surface - back_temp)
    )
    slope = film + 4.0 * radiation * emissivity * cubed + conduction
    return surface + imbalance / slope


def lanes(shape):
    return lax.broadcasted_iota(jnp.int32, shape, len(shape) - 1)


def rows(shape):
    return lax.broadcasted_iota(jnp.int32, shape, len(shape) - 2)


def spot(x):
    return (x + 4) % 5, (x + 4) // 5


def kernel(
    recovery_temp, film_coeff, emissivity, char_density, back_temp, stencil_frac,
    wall_owner, stencil_start, live_count, wall_mask, wall_dir, stiffness, start_disp,
    surface_out, disp_out,
    recovery_v, film_v, emissivity_v, char_v, back_v, frac_v, owner_v, start_v, live_v, mask_v, dir_v, surface_v,
    planes, strip_up, strip_down, strip_from_below, strip_from_above,
    slab_up, slab_down, slab_below, slab_above, edge_send, edge_recv, cross_send, cross_recv,
    ends, halos, weights, field_a, field_b, result,
    side_weights, side_a, side_b, side_source,
    dep_send, dep_recv, ghost, ghost_cross, ghost_side, ghost_face, ghost_corner, ghost_all,
    local_sem, send_sem, recv_sem, dep_sem,
):
    gx, gy, gz = (lax.axis_index(a) for a in ("gx", "gy", "gz"))
    position = (gx, gy, gz)
    limits = (SIZES["gx"], SIZES["gy"], SIZES["gz"])

    def there(step):
        found = None
        for p, d, n in zip(position, step, limits):
            if d != 0:
                ok = (p + d >= 0) & (p + d < n)
                found = ok if found is None else found & ok
        return found

    def target(step):
        return tuple(p + d for p, d in zip(position, step))

    def back(step):
        return tuple(-d for d in step)

    on_wall = gz == 0

    class Message:
        def __init__(self, channel, step, src, dst, walls=False):
            self.to, self.origin = there(step), there(back(step))
            if walls:
                self.to, self.origin = self.to & on_wall, self.origin & on_wall
            self.copy = pltpu.make_async_remote_copy(
                src_ref=src, dst_ref=dst, send_sem=send_sem.at[channel], recv_sem=recv_sem.at[channel],
                device_id=target(step), device_id_type=MESH,
            )

        def start(self):
            pl.when(self.to)(self.copy.start)

        def wait_recv(self):
            pl.when(self.origin)(self.copy.wait_recv)

        def wait_send(self):
            pl.when(self.to)(self.copy.wait_send)

    small = [
        pltpu.make_async_copy(src, dst, local_sem.at[8 + k])
        for k, (src, dst) in enumerate((
            (recovery_temp, recovery_v), (film_coeff, film_v), (emissivity, emissivity_v), (char_density, char_v),
            (back_temp, back_v), (stencil_frac, frac_v), (wall_owner, owner_v), (stencil_start, start_v),
            (live_count, live_v), (wall_mask, mask_v), (wall_dir, dir_v),
        ))
    ]
    for copy in small:
        copy.start()
    load_u = pltpu.make_async_copy(start_disp, planes.at[0:3, 4:36, 0:32], local_sem.at[0])
    load_k = pltpu.make_async_copy(stiffness, planes.at[3, 4:36, 0:32], local_sem.at[1])
    load_u.start()
    load_k.start()

    barrier = pltpu.get_barrier_semaphore()
    near = [(1, 0, 0), (-1, 0, 0), (0, 1, 0), (0, -1, 0), (0, 0, 1), (0, 0, -1)]
    near += [(0, a, b) for a in (1, -1) for b in (1, -1)]
    corners = [(a, b, 0) for a in (1, -1) for b in (1, -1)]
    expected = jnp.where(on_wall, 3, 4)

    def greet(step, ok):
        pl.when(ok)(lambda: pl.semaphore_signal(barrier, inc=1, device_id=target(step), device_id_type=MESH))
        return ok.astype(jnp.int32)

    for step in near:
        expected = expected + greet(step, there(step))
    for step in corners:
        expected = expected + greet(step, there(step) & on_wall)
    rank = gy * limits[2] + gz
    for y in range(limits[1]):
        for z in range(limits[2]):
            pl.when(on_wall & (rank != y * limits[2] + z))(
                lambda y=y, z=z: pl.semaphore_signal(barrier, inc=1, device_id=(gx, y, z), device_id_type=MESH)
            )

    for copy in small:
        copy.wait()
    back_t = back_v[...]
    surface = back_t
    for _ in range(NEWTON):
        surface = balance_step(surface, recovery_v[...], film_v[...], emissivity_v[...], back_t)
    surface_v[...] = surface
    surface_copy = pltpu.make_async_copy(surface_v, surface_out, local_sem.at[7])
    surface_copy.start()
    recession = time_step * ablation_rate(surface) / char_v[...]
    shape = (32, 128)
    lane = lanes(shape)
    square = (32, 32)
    diagonal = rows(square) == lanes(square)

    def column(row):
        spread = jnp.broadcast_to(row.astype(F32), square)
        return jnp.broadcast_to(jnp.sum(jnp.where(diagonal, spread, 0.0), axis=1, keepdims=True), shape)

    starts = start_v[...]
    shift = column(starts & 127)
    live = lane.astype(F32) < column(live_v[...])
    upper = jnp.where(live, frac_v[...], 0.0)
    lower = jnp.where(live, 1.0 - frac_v[...], 0.0)
    shift = shift.astype(jnp.int32)
    first, second = [], []
    for low, high in ((lower * recession, upper * recession), (lower, upper)):
        moved = pltpu.roll(high, 1, axis=1)
        spread = low + jnp.where(lane >= 1, moved, 0.0)
        last = jnp.broadcast_to(moved[:, 0:1], shape)
        for bit in range(7):
            spread = jnp.where(((shift >> bit) & 1) == 1, pltpu.roll(spread, 1 << bit, axis=1), spread)
        first.append(jnp.where(lane >= shift, spread, 0.0))
        second.append(jnp.where(lane < shift, spread, jnp.where(lane == shift, last, 0.0)))
    face_row = owner_v[...] * 8
    row_a = jnp.broadcast_to(face_row + (starts >> 7), square)
    row_b = jnp.broadcast_to(face_row + (((starts >> 7) + 1) & 7), square)

    def gathered(row, terms):
        pick = (rows(square) == row).astype(F32)
        return jnp.dot(pick, terms, precision=lax.Precision.HIGHEST, preferred_element_type=F32)

    summed = gathered(row_a, jnp.concatenate(first, axis=1)) + gathered(row_b, jnp.concatenate(second, axis=1))
    for o in range(4):
        dep_send[o, 0:8] = summed[8 * o : 8 * o + 8, 0:128]
        dep_send[o, 8:16] = summed[8 * o : 8 * o + 8, 128:256]

    tile = (8, 128)
    top = rows(tile) < 4
    tile_lane = lanes(tile)
    load_u.wait()
    load_k.wait()

    def group(lane):
        return ((lane + 4) & 127) // 16

    def pack_ends(c, x_list, first, count, keep):
        size = (count, 128)
        where = group(lanes(size))
        for i in range(5):
            found = [x for x in x_list if spot(x)[0] == i]
            packed = ends[c, i, first : first + count] if keep else jnp.zeros(size, F32)
            for x in found:
                turned = pltpu.roll(planes[c, x + 4, first : first + count], 16 * spot(x)[1] + 4, axis=1)
                packed = jnp.where(where == spot(x)[1], turned, packed)
            if found or not keep:
                ends[c, i, first : first + count] = packed

    inside = range(32)
    outside = (-4, -3, -2, -1, 32, 33, 34, 35)

    def pack_own(c, _):
        pack_ends(c, inside, 0, 32, False)
        return 0

    lax.fori_loop(0, 4, pack_own, 0)
    quarter = lanes(shape) % 16 // 4
    for i in range(5):
        up, down = jnp.zeros(shape, F32), jnp.zeros(shape, F32)
        for c in range(4):
            both = ends[c, i, 0:32]
            up = jnp.where(quarter == c, pltpu.roll(both, 4 * c, axis=1) if c else both, up)
            down = jnp.where(quarter == c, pltpu.roll(both, (4 * c - 4) % 128, axis=1) if c != 1 else both, down)
        slab_up[i] = up
        slab_down[i] = down

    def rows_down(a, b):
        return jnp.where(top, a, pltpu.roll(b, 4, axis=0))

    def rows_up(a, b):
        return jnp.where(top, pltpu.roll(b, 4, axis=0), a)

    def pack_y(x, _):
        for pair in range(2):
            a, b = 2 * pair, 2 * pair + 1
            strip_down[pair, x] = rows_down(planes[a, x + 4, 0:8], planes[b, x + 4, 0:8])
            strip_up[pair, x] = rows_up(planes[a, x + 4, 24:32], planes[b, x + 4, 24:32])
        return 0

    lax.fori_loop(0, 32, pack_y, 0)
    for pair in range(3):
        a, b = 2 * pair, min(2 * pair + 1, 4)
        edge_send[0, pair] = rows_down(slab_up[a, 0:8], slab_up[b, 0:8])
        edge_send[1, pair] = rows_up(slab_up[a, 24:32], slab_up[b, 24:32])
        edge_send[2, pair] = rows_down(slab_down[a, 0:8], slab_down[b, 0:8])
        edge_send[3, pair] = rows_up(slab_down[a, 24:32], slab_down[b, 24:32])

    east, west, north, south = (1, 0, 0), (-1, 0, 0), (0, 1, 0), (0, -1, 0)
    x_far = [
        Message(0, east, start_disp.at[:, 28:32], planes.at[0:3, 0:4, 0:32]),
        Message(1, east, stiffness.at[28:32], planes.at[3, 0:4, 0:32]),
        Message(2, west, start_disp.at[:, 0:4], planes.at[0:3, 36:40, 0:32]),
        Message(3, west, stiffness.at[0:4], planes.at[3, 36:40, 0:32]),
    ]
    y_far = [Message(4, north, strip_up, strip_from_below), Message(5, south, strip_down, strip_from_above)]
    z_far = [
        Message(6, (0, 0, 1), slab_up, slab_below.at[:, 0:32]),
        Message(7, (0, 0, -1), slab_down, slab_above.at[:, 0:32]),
    ]
    edges = [
        Message(8, (0, -1, 1), edge_send.at[0], edge_recv.at[0]),
        Message(9, (0, 1, 1), edge_send.at[1], edge_recv.at[1]),
        Message(10, (0, -1, -1), edge_send.at[2], edge_recv.at[2]),
        Message(11, (0, 1, -1), edge_send.at[3], edge_recv.at[3]),
    ]

    pl.semaphore_wait(barrier, expected)

    def deposit_copy(y):
        ahead = lax.rem(rank - y * limits[2] + 32, 32)
        slot = jnp.maximum(ahead - 1, 0)
        copy = pltpu.make_async_remote_copy(
            src_ref=dep_send.at[y], dst_ref=dep_recv.at[slot], send_sem=send_sem.at[24 + y], recv_sem=dep_sem.at[0],
            device_id=(gx, y, 0), device_id_type=MESH,
        )
        return ahead != 0, copy

    for message in y_far + z_far + edges:
        message.start()
    for y in range(4):
        away, copy = deposit_copy(y)
        pl.when(away)(copy.start)
    for message in x_far:
        message.start()

    def clear(step, *refs):
        @pl.when(jnp.logical_not(there(step)))
        def _():
            for ref in refs:
                ref[...] = jnp.zeros(ref.shape, F32)

    clear(north, strip_from_above)
    clear(south, strip_from_below)
    clear((0, 0, -1), slab_below.at[:, 0:32])
    clear((0, 0, 1), slab_above.at[:, 0:32])
    for k, message_step in enumerate(((0, -1, 1), (0, 1, 1), (0, -1, -1), (0, 1, -1))):
        clear(back(message_step), edge_recv.at[k])
    clear(west, planes.at[:, 0:4, 0:32], planes.at[:, 1:4, 32:40], cross_recv.at[0])
    clear(east, planes.at[:, 36:40, 0:32], planes.at[:, 36:39, 32:40], cross_recv.at[1])
    planes[:, 0, 32:40] = jnp.zeros((4, 8, 128), F32)
    planes[:, 39, 32:40] = jnp.zeros((4, 8, 128), F32)

    for message in y_far:
        message.wait_recv()

    def merged(from_above, from_below):
        a = jnp.where(top, from_above, from_below)
        b = pltpu.roll(jnp.where(top, from_below, from_above), 4, axis=0)
        return a, b

    def merge_y(x, _):
        for pair in range(2):
            a, b = merged(strip_from_above[pair, x], strip_from_below[pair, x])
            planes[2 * pair, x + 4, 32:40] = a
            planes[2 * pair + 1, x + 4, 32:40] = b
        return 0

    lax.fori_loop(0, 32, merge_y, 0)
    x_rows = [
        Message(12, east, planes.at[:, 33:36, 32:40], planes.at[:, 1:4, 32:40]),
        Message(13, west, planes.at[:, 4:7, 32:40], planes.at[:, 36:39, 32:40]),
    ]
    for message in x_rows:
        message.start()

    for message in z_far + edges:
        message.wait_recv()
    for pair in range(3):
        a, b = merged(edge_recv[0, pair], edge_recv[1, pair])
        slab_below[2 * pair, 32:40] = a
        if pair < 2:
            slab_below[2 * pair + 1, 32:40] = b
        a, b = merged(edge_recv[2, pair], edge_recv[3, pair])
        slab_above[2 * pair, 32:40] = a
        if pair < 2:
            slab_above[2 * pair + 1, 32:40] = b
    tall = (EXT, 128)
    sixteen = lanes(tall) // 16
    far_x = ((28, 29, 30, 31), (0, 1, 2, 3))
    halo_x = ((-4, -3, -2, -1), (32, 33, 34, 35))
    for d in range(2):
        cross = jnp.zeros(tall, F32)
        for k, x in enumerate(far_x[d]):
            i, g = spot(x)
            cross = jnp.where(sixteen == k, pltpu.roll(slab_below[i], (16 * (k - g)) % 128, axis=1), cross)
            cross = jnp.where(sixteen == 4 + k, pltpu.roll(slab_above[i], (16 * (4 + k - g)) % 128, axis=1), cross)
        cross_send[d] = cross
    x_cross = [
        Message(14, east, cross_send.at[0], cross_recv.at[0]),
        Message(15, west, cross_send.at[1], cross_recv.at[1]),
    ]
    for message in x_cross:
        message.start()

    def spread(c, X, j):
        return planes[c, X, pl.ds(j, 8, stride=5), :]

    def beside_y(read, c, X, j):
        above = read(c, X, j + 1) if j < 4 else pltpu.roll(read(c, X, 0), 7, axis=0)
        below = read(c, X, j - 1) if j > 0 else pltpu.roll(read(c, X, 4), 1, axis=0)
        return above, below

    def weigh(X):
        for j in range(5):
            centre = spread(3, X, j)
            above, below = beside_y(spread, 3, X, j)
            sides = (
                spread(3, X + 1, j), spread(3, X - 1, j), above, below,
                pltpu.roll(centre, 127, axis=1), pltpu.roll(centre, 1, axis=1),
            )
            weight = 6.0 * centre
            for side in sides:
                weight = weight + side
            inverse = jnp.where(centre > 0.0, 1.0 / weight, 0.0)
            for n, side in enumerate(sides):
                weights[n, X, j] = (centre + side) * inverse

    def reader(field):
        return lambda c, X, j: field[c, X, j]

    def to_field(field):
        def write(c, X, j, value):
            field[c, X, j] = value

        return write

    def to_result(c, X, j, value):
        result[c, X - 4, pl.ds(j, 8, stride=5), :] = value

    def relax(read, write, X):
        for j in range(5):
            w = [weights[n, X, j] for n in range(6)]
            for c in range(3):
                centre = read(c, X, j)
                above, below = beside_y(read, c, X, j)
                total = w[0] * read(c, X + 1, j) + w[1] * read(c, X - 1, j)
                total = total + (w[2] * above + w[3] * below)
                total = total + (w[4] * pltpu.roll(centre, 127, axis=1) + w[5] * pltpu.roll(centre, 1, axis=1))
                write(c, X, j, total)

    def span(body, start, stop, many):
        def step(k, _):
            first = jnp.minimum(start + k * many, stop - many)
            for n in range(many):
                body(first + n)
            return 0

        lax.fori_loop(0, -(-(stop - start) // many), step, 0)

    stages = (
        (spread, to_field(field_a)), (reader(field_a), to_field(field_b)),
        (reader(field_b), to_field(field_a)), (reader(field_a), to_result),
    )
    MANY = 4
    span(weigh, 5, 35, 2)
    for sweep, (read, write) in enumerate(stages):
        span(lambda X, read=read, write=write: relax(read, write, X), 5 + sweep, 35 - sweep, MANY)

    @pl.when(on_wall)
    def _():
        everyone = pltpu.make_async_remote_copy(
            src_ref=dep_recv, dst_ref=dep_recv, send_sem=send_sem.at[24], recv_sem=dep_sem.at[0],
            device_id=(gx, 0, 0), device_id_type=MESH,
        )
        everyone.wait_recv()
        total = dep_send[gy]
        for k in range(31):
            total = total + dep_recv[k]
        face = total[0:8] / (1.0 + total[8:16])
        wide = (8, 640)
        at = lanes(wide)
        which = 5 * (at % 128 // 16) + at // 128 - 4
        acc = jnp.zeros((96, 640), F32)
        for q in range(4):
            mask = mask_v[pl.ds(q, 8, stride=4), :].astype(F32)
            part = face[:, 32 * q : 32 * q + 32] * (-mask)
            values = jnp.concatenate([part * dir_v[c, pl.ds(q, 8, stride=4), :] for c in range(3)], axis=1)
            pick = ((at % 16 == 3) & (which == 4 * rows(wide) + q)).astype(F32)
            acc = acc + lax.dot_general(
                values, pick, (((0,), (0,)), ((), ())), precision=lax.Precision.HIGHEST, preferred_element_type=F32
            )
        short = (32, 128)
        eighth = lanes(short) // 16
        for c in range(3):
            own = [acc[32 * c : 32 * c + 32, 128 * i : 128 * i + 128] for i in range(5)]
            for i in range(5):
                ghost[i, c] = own[i]
            for d in range(2):
                cross = jnp.zeros(short, F32)
                for k, x in enumerate(far_x[d]):
                    i, g = spot(x)
                    cross = jnp.where(eighth == k, pltpu.roll(own[i], (16 * (k - g)) % 128, axis=1), cross)
                ghost_cross[d, c] = cross

    g_side = [
        Message(16, north, ghost.at[:, :, 24:32], ghost_side.at[0], True),
        Message(17, south, ghost.at[:, :, 0:8], ghost_side.at[1], True),
    ]
    g_face = [
        Message(18, east, ghost_cross.at[0], ghost_face.at[0], True),
        Message(19, west, ghost_cross.at[1], ghost_face.at[1], True),
    ]
    g_corner = [
        Message(20, (1, 1, 0), ghost_cross.at[0, :, 24:32], ghost_corner.at[0], True),
        Message(21, (1, -1, 0), ghost_cross.at[0, :, 0:8], ghost_corner.at[1], True),
        Message(22, (-1, 1, 0), ghost_cross.at[1, :, 24:32], ghost_corner.at[2], True),
        Message(23, (-1, -1, 0), ghost_cross.at[1, :, 0:8], ghost_corner.at[3], True),
    ]
    g_all = g_side + g_face + g_corner
    for message in g_all:
        message.start()
    clear(south, ghost_side.at[0])
    clear(north, ghost_side.at[1])
    clear(west, ghost_face.at[0])
    clear(east, ghost_face.at[1])
    for k, step in enumerate(((1, 1, 0), (1, -1, 0), (-1, 1, 0), (-1, -1, 0))):
        clear(back(step), ghost_corner.at[k])

    for message in x_far + x_rows:
        message.wait_recv()
    span(weigh, 1, 5, 2)
    span(weigh, 35, 39, 2)
    for sweep, (read, write) in enumerate(stages):
        span(lambda X, read=read, write=write: relax(read, write, X), 1 + sweep, 5 + sweep, 4)
        span(lambda X, read=read, write=write: relax(read, write, X), 35 - sweep, 39 - sweep, 4)

    for message in x_cross:
        message.wait_recv()

    def pack_rest(c, _):
        pack_ends(c, inside, 32, 8, False)
        pack_ends(c, outside, 0, 32, True)
        pack_ends(c, outside, 32, 8, True)
        return 0

    lax.fori_loop(0, 4, pack_rest, 0)
    for d in range(2):
        for k, x in enumerate(halo_x[d]):
            i, g = spot(x)
            from_below = pltpu.roll(cross_recv[d], (16 * (g - k)) % 128, axis=1)
            from_above = pltpu.roll(cross_recv[d], (16 * (g - 4 - k)) % 128, axis=1)
            slab_below[i] = jnp.where(sixteen == g, from_below, slab_below[i])
            slab_above[i] = jnp.where(sixteen == g, from_above, slab_above[i])
    place = lanes(tall) % 16
    for c in range(4):
        for i in range(5):
            under = pltpu.roll(slab_below[i], (128 - 4 * c) % 128, axis=1) if c else slab_below[i]
            over = pltpu.roll(slab_above[i], (4 - 4 * c) % 128, axis=1) if c != 1 else slab_above[i]
            halos[c, i] = jnp.where(place < 4, under, jnp.where(place < 8, over, 0.0))

    side_source[...] = jnp.zeros(side_source.shape, F32)

    @pl.when(on_wall)
    def _():
        for message in g_all:
            message.wait_recv()
        eighth = lanes((32, 128)) // 16
        eighth_tile = tile_lane // 16
        for c in range(3):
            whole = [ghost[i, c] for i in range(5)]
            rest = [jnp.where(top, ghost_side[1, i, c], ghost_side[0, i, c]) for i in range(5)]
            for d in range(2):
                face = ghost_face[d, c]
                corner = jnp.where(top, ghost_corner[2 * d + 1, c], ghost_corner[2 * d, c])
                for k, x in enumerate(halo_x[d]):
                    i, g = spot(x)
                    whole[i] = jnp.where(eighth == g, pltpu.roll(face, (16 * (g - k)) % 128, axis=1), whole[i])
                    rest[i] = jnp.where(eighth_tile == g, pltpu.roll(corner, (16 * (g - k)) % 128, axis=1), rest[i])
            for i in range(5):
                ghost_all[c, i, 0:32] = whole[i]
                ghost_all[c, i, 32:40] = rest[i]
        for c in range(3):
            for i in range(5):
                for j in range(5):
                    side_source[c, i, j] = ghost_all[c, i, pl.ds(j, 8, stride=5), :]

    tile_place = tile_lane % 16
    low_end = (tile_place >= 4) & (tile_place < 12)
    high_end = (tile_place >= 12) | (tile_place < 4)

    def side_raw(step, _):
        c, i = lax.div(step, 5), lax.rem(step, 5)
        for j in range(5):
            own = ends[c, i, pl.ds(j, 8, stride=5), :]
            halo = halos[c, i, pl.ds(j, 8, stride=5), :]
            low = jnp.where(low_end, own, halo)
            side_a[0, c, i, j] = low
            side_a[1, c, i, j] = jnp.where(high_end, own, halo)
        return 0

    lax.fori_loop(0, 20, side_raw, 0)
    for c in range(3):
        for i in range(5):
            for j in range(5):
                side_a[0, c, i, j] = side_a[0, c, i, j] + side_source[c, i, j]

    def side_sides(field, e, c, i, j):
        here = field[e, c, i, j]
        return (
            field[e, c, i + 1, j] if i < 4 else pltpu.roll(field[e, c, 0, j], 112, axis=1),
            field[e, c, i - 1, j] if i > 0 else pltpu.roll(field[e, c, 4, j], 16, axis=1),
            field[e, c, i, j + 1] if j < 4 else pltpu.roll(field[e, c, i, 0], 7, axis=0),
            field[e, c, i, j - 1] if j > 0 else pltpu.roll(field[e, c, i, 4], 1, axis=0),
            pltpu.roll(here, 127, axis=1),
            pltpu.roll(here, 1, axis=1),
        )

    def side_weigh(e, _):
        for i in range(5):
            for j in range(5):
                centre = side_a[e, 3, i, j]
                sides = side_sides(side_a, e, 3, i, j)
                weight = 6.0 * centre
                for side in sides:
                    weight = weight + side
                inverse = jnp.where(centre > 0.0, 1.0 / weight, 0.0)
                for n, side in enumerate(sides):
                    side_weights[n, e, i, j] = (centre + side) * inverse
        return 0

    lax.fori_loop(0, 2, side_weigh, 0)
    for sweep in range(SWEEPS):
        src, dst = (side_a, side_b) if sweep % 2 == 0 else (side_b, side_a)
        for e in range(2):

            def side_relax(c, _, src=src, dst=dst, e=e):
                for i in range(5):
                    for j in range(5):
                        sides = side_sides(src, e, c, i, j)
                        total = side_weights[0, e, i, j] * sides[0]
                        for n in range(1, 6):
                            total = total + side_weights[n, e, i, j] * sides[n]
                        dst[e, c, i, j] = total + side_source[c, i, j] if e == 0 else total
                return 0

            lax.fori_loop(0, 3, side_relax, 0)

    edge_lane = (tile_lane < 4) | (tile_lane >= 124)
    outs = []
    for c in range(3):

        def put_back(j, _, c=c):
            for i in range(5):
                both = jnp.where(tile_place < 4, side_a[1, c, i, j], side_a[0, c, i, j])
                for x in inside:
                    if spot(x)[0] == i:
                        turned = pltpu.roll(both, 128 - 16 * spot(x)[1] - 4, axis=1)
                        here = pl.ds(j, 8, stride=5)
                        result[c, x, here, :] = jnp.where(edge_lane, turned, result[c, x, here, :])
            return 0

        lax.fori_loop(0, 5, put_back, 0)
        copy = pltpu.make_async_copy(result.at[c, :, 0:32], disp_out.at[c], local_sem.at[2 + c])
        copy.start()
        outs.append(copy)

    for message in x_far + y_far + z_far + edges + x_rows + x_cross + g_all:
        message.wait_send()
    for y in range(4):
        away, copy = deposit_copy(y)
        pl.when(away)(copy.wait_send)
    for copy in outs:
        copy.wait()
    surface_copy.wait()


def local(
    recovery_temp, film_coeff, emissivity, char_density, back_temp, stencil_frac,
    wall_owner, stencil_start, live_count, wall_mask, wall_dir, stiffness, start_disp,
):
    hbm = pl.BlockSpec(memory_space=pl.ANY)
    def f32(*shape):
        return pltpu.VMEM(shape, F32)

    def i32(*shape):
        return pltpu.VMEM(shape, jnp.int32)

    scratch = [f32(32, 128)] * 6 + [i32(1, 32)] * 3 + [i32(32, 32), f32(3, 32, 32), f32(32, 128)]
    scratch += [
        f32(4, EXT, EXT, 128),
        f32(2, 32, 8, 128),
        f32(2, 32, 8, 128),
        f32(2, 32, 8, 128),
        f32(2, 32, 8, 128),
        f32(5, 32, 128),
        f32(5, 32, 128),
        f32(5, EXT, 128),
        f32(5, EXT, 128),
        f32(4, 3, 8, 128),
        f32(4, 3, 8, 128),
        f32(2, EXT, 128),
        f32(2, EXT, 128),
        f32(4, 5, EXT, 128),
        f32(4, 5, EXT, 128),
        f32(6, EXT, 5, 8, 128),
        f32(3, EXT, 5, 8, 128),
        f32(3, EXT, 5, 8, 128),
        f32(3, 32, EXT, 128),
        f32(6, 2, 5, 5, 8, 128),
        f32(2, 4, 5, 5, 8, 128),
        f32(2, 3, 5, 5, 8, 128),
        f32(3, 5, 5, 8, 128),
        f32(4, 16, 128),
        f32(31, 16, 128),
        f32(5, 3, 32, 128),
        f32(2, 3, 32, 128),
        f32(2, 5, 3, 8, 128),
        f32(2, 3, 32, 128),
        f32(4, 3, 8, 128),
        f32(3, 5, EXT, 128),
    ]
    return pl.pallas_call(
        kernel,
        out_shape=(
            jax.ShapeDtypeStruct(back_temp.shape, F32),
            jax.ShapeDtypeStruct(start_disp.shape, F32),
        ),
        in_specs=[hbm] * 13,
        out_specs=(hbm, hbm),
        scratch_shapes=scratch
        + [
            pltpu.SemaphoreType.DMA((19,)),
            pltpu.SemaphoreType.DMA((28,)),
            pltpu.SemaphoreType.DMA((24,)),
            pltpu.SemaphoreType.DMA((1,)),
        ],
        compiler_params=pltpu.CompilerParams(collective_id=0, has_side_effects=True, vmem_limit_bytes=60 << 20),
    )(
        recovery_temp, film_coeff, emissivity, char_density, back_temp, stencil_frac,
        wall_owner.reshape(1, 32), stencil_start.reshape(1, 32), live_count.reshape(1, 32),
        wall_mask, wall_dir, stiffness, start_disp,
    )


def solution(mesh):
    tiles = P(("gx", "gy", "gz"), None)
    flat = P(("gx", "gy", "gz"))
    in_specs = (tiles,) * 7 + (flat, flat, P("gx", "gy"), P(None, "gx", "gy"), P("gx", "gy", "gz"), P(None, "gx", "gy", "gz"))
    out_specs = (tiles, P(None, "gx", "gy", "gz"))
    return jax.shard_map(local, mesh=mesh, in_specs=in_specs, out_specs=out_specs, check_vma=False)
```

```python
import jax
import jax.numpy as jnp
from jax import lax
from jax.experimental import pallas as pl
from jax.experimental.pallas import tpu as pltpu
from jax.sharding import PartitionSpec as P

NEWTON = 6
SWEEPS = 4
MESH = pl.DeviceIdType.MESH
F32 = jnp.float32
SIZES = {"gx": 8, "gy": 4, "gz": 8}
EXT = 40

arrhenius_scale = 0.5
activation = 3.0
blowing = 0.5
heat_release = 0.3
radiation = 0.05
conduction = 0.5
time_step = 1.5


def ablation_rate(surface):
    return arrhenius_scale * jnp.exp(activation * (1.0 - 1.0 / surface))


def balance_step(surface, recovery_temp, film_coeff, emissivity, back_temp):
    ablate = ablation_rate(surface)
    film = film_coeff * film_coeff / (film_coeff + blowing * ablate)
    cubed = surface * surface * surface
    imbalance = (
        film * (recovery_temp - surface)
        + heat_release * ablate
        - radiation * emissivity * (cubed * surface)
        - conduction * (surface - back_temp)
    )
    slope = film + 4.0 * radiation * emissivity * cubed + conduction
    return surface + imbalance / slope


def lanes(shape):
    return lax.broadcasted_iota(jnp.int32, shape, len(shape) - 1)


def rows(shape):
    return lax.broadcasted_iota(jnp.int32, shape, len(shape) - 2)


def spot(x):
    return (x + 4) % 5, (x + 4) // 5


def kernel(
    recovery_temp, film_coeff, emissivity, char_density, back_temp, stencil_frac,
    wall_owner, stencil_start, live_count, wall_mask, wall_dir, stiffness, start_disp,
    surface_out, disp_out,
    recovery_v, film_v, emissivity_v, char_v, back_v, frac_v, owner_v, start_v, live_v, mask_v, dir_v,
    planes, strip_up, strip_down, strip_from_below, strip_from_above,
    slab_up, slab_down, slab_below, slab_above, edge_send, edge_recv, cross_send, cross_recv,
    ends, halos, weights, field_a, field_b, result,
    side_weights, side_a, side_b, side_source,
    dep_send, dep_recv, ghost, ghost_cross, ghost_side, ghost_face, ghost_corner, ghost_all,
    local_sem, send_sem, recv_sem, dep_sem,
):
    gx, gy, gz = (lax.axis_index(a) for a in ("gx", "gy", "gz"))
    position = (gx, gy, gz)
    limits = (SIZES["gx"], SIZES["gy"], SIZES["gz"])

    def there(step):
        found = None
        for p, d, n in zip(position, step, limits):
            if d != 0:
                ok = (p + d >= 0) & (p + d < n)
                found = ok if found is None else found & ok
        return found

    def target(step):
        return tuple(p + d for p, d in zip(position, step))

    def back(step):
        return tuple(-d for d in step)

    on_wall = gz == 0

    class Message:
        def __init__(self, channel, step, src, dst, walls=False):
            self.to, self.origin = there(step), there(back(step))
            if walls:
                self.to, self.origin = self.to & on_wall, self.origin & on_wall
            self.copy = pltpu.make_async_remote_copy(
                src_ref=src, dst_ref=dst, send_sem=send_sem.at[channel], recv_sem=recv_sem.at[channel],
                device_id=target(step), device_id_type=MESH,
            )

        def start(self):
            pl.when(self.to)(self.copy.start)

        def wait_recv(self):
            pl.when(self.origin)(self.copy.wait_recv)

        def wait_send(self):
            pl.when(self.to)(self.copy.wait_send)

    small = [
        pltpu.make_async_copy(src, dst, local_sem.at[8 + k])
        for k, (src, dst) in enumerate((
            (recovery_temp, recovery_v), (film_coeff, film_v), (emissivity, emissivity_v), (char_density, char_v),
            (back_temp, back_v), (stencil_frac, frac_v), (wall_owner, owner_v), (stencil_start, start_v),
            (live_count, live_v), (wall_mask, mask_v), (wall_dir, dir_v),
        ))
    ]
    for copy in small:
        copy.start()
    load_u = pltpu.make_async_copy(start_disp, planes.at[0:3, 4:36, 0:32], local_sem.at[0])
    load_k = pltpu.make_async_copy(stiffness, planes.at[3, 4:36, 0:32], local_sem.at[1])
    load_u.start()
    load_k.start()

    barrier = pltpu.get_barrier_semaphore()
    near = [(1, 0, 0), (-1, 0, 0), (0, 1, 0), (0, -1, 0), (0, 0, 1), (0, 0, -1)]
    near += [(0, a, b) for a in (1, -1) for b in (1, -1)]
    corners = [(a, b, 0) for a in (1, -1) for b in (1, -1)]
    expected = jnp.where(on_wall, 3, 4)

    def greet(step, ok):
        pl.when(ok)(lambda: pl.semaphore_signal(barrier, inc=1, device_id=target(step), device_id_type=MESH))
        return ok.astype(jnp.int32)

    for step in near:
        expected = expected + greet(step, there(step))
    for step in corners:
        expected = expected + greet(step, there(step) & on_wall)
    rank = gy * limits[2] + gz
    for y in range(limits[1]):
        for z in range(limits[2]):
            pl.when(on_wall & (rank != y * limits[2] + z))(
                lambda y=y, z=z: pl.semaphore_signal(barrier, inc=1, device_id=(gx, y, z), device_id_type=MESH)
            )

    tile = (8, 128)
    top = rows(tile) < 4
    tile_lane = lanes(tile)
    load_u.wait()
    load_k.wait()

    def rows_down(a, b):
        return jnp.where(top, a, pltpu.roll(b, 4, axis=0))

    def rows_up(a, b):
        return jnp.where(top, pltpu.roll(b, 4, axis=0), a)

    def pack_y(k, _):
        for x in (8 * k + n for n in range(8)):
            for pair in range(2):
                a, b = 2 * pair, 2 * pair + 1
                strip_down[pair, x] = rows_down(planes[a, x + 4, 0:8], planes[b, x + 4, 0:8])
                strip_up[pair, x] = rows_up(planes[a, x + 4, 24:32], planes[b, x + 4, 24:32])
        return 0

    lax.fori_loop(0, 4, pack_y, 0)
    east, west, north, south = (1, 0, 0), (-1, 0, 0), (0, 1, 0), (0, -1, 0)
    x_far = [
        Message(0, east, start_disp.at[:, 28:32], planes.at[0:3, 0:4, 0:32]),
        Message(1, east, stiffness.at[28:32], planes.at[3, 0:4, 0:32]),
        Message(2, west, start_disp.at[:, 0:4], planes.at[0:3, 36:40, 0:32]),
        Message(3, west, stiffness.at[0:4], planes.at[3, 36:40, 0:32]),
    ]
    y_far = [Message(4, north, strip_up, strip_from_below), Message(5, south, strip_down, strip_from_above)]
    z_far = [
        Message(6, (0, 0, 1), slab_up, slab_below.at[:, 0:32]),
        Message(7, (0, 0, -1), slab_down, slab_above.at[:, 0:32]),
    ]
    edges = [
        Message(8, (0, -1, 1), edge_send.at[0], edge_recv.at[0]),
        Message(9, (0, 1, 1), edge_send.at[1], edge_recv.at[1]),
        Message(10, (0, -1, -1), edge_send.at[2], edge_recv.at[2]),
        Message(11, (0, 1, -1), edge_send.at[3], edge_recv.at[3]),
    ]

    pl.semaphore_wait(barrier, expected)

    def deposit_copy(y):
        ahead = lax.rem(rank - y * limits[2] + 32, 32)
        slot = jnp.maximum(ahead - 1, 0)
        copy = pltpu.make_async_remote_copy(
            src_ref=dep_send.at[y], dst_ref=dep_recv.at[slot], send_sem=send_sem.at[24 + y], recv_sem=dep_sem.at[0],
            device_id=(gx, y, 0), device_id_type=MESH,
        )
        return ahead != 0, copy

    for message in y_far + x_far:
        message.start()

    for copy in small:
        copy.wait()
    back_t = back_v[...]
    surface = back_t
    for _ in range(NEWTON):
        surface = balance_step(surface, recovery_v[...], film_v[...], emissivity_v[...], back_t)
    surface_out[...] = surface
    recession = time_step * ablation_rate(surface) / char_v[...]
    shape = (32, 128)
    lane = lanes(shape)
    square = (32, 32)
    diagonal = rows(square) == lanes(square)

    def column(row):
        spread = jnp.broadcast_to(row.astype(F32), square)
        return jnp.broadcast_to(jnp.sum(jnp.where(diagonal, spread, 0.0), axis=1, keepdims=True), shape)

    starts = start_v[...]
    shift = column(starts & 127)
    live = lane.astype(F32) < column(live_v[...])
    upper = jnp.where(live, frac_v[...], 0.0)
    lower = jnp.where(live, 1.0 - frac_v[...], 0.0)
    shift = shift.astype(jnp.int32)
    first, second = [], []
    for low, high in ((lower * recession, upper * recession), (lower, upper)):
        moved = pltpu.roll(high, 1, axis=1)
        spread = low + jnp.where(lane >= 1, moved, 0.0)
        last = jnp.broadcast_to(moved[:, 0:1], shape)
        for bit in range(7):
            spread = jnp.where(((shift >> bit) & 1) == 1, pltpu.roll(spread, 1 << bit, axis=1), spread)
        first.append(jnp.where(lane >= shift, spread, 0.0))
        second.append(jnp.where(lane < shift, spread, jnp.where(lane == shift, last, 0.0)))
    face_row = owner_v[...] * 8
    row_a = jnp.broadcast_to(face_row + (starts >> 7), square)
    row_b = jnp.broadcast_to(face_row + (((starts >> 7) + 1) & 7), square)

    def gathered(row, terms):
        pick = (rows(square) == row).astype(F32)
        return jnp.dot(pick, terms, precision=lax.Precision.HIGHEST, preferred_element_type=F32)

    summed = gathered(row_a, jnp.concatenate(first, axis=1)) + gathered(row_b, jnp.concatenate(second, axis=1))
    for o in range(4):
        dep_send[o, 0:8] = summed[8 * o : 8 * o + 8, 0:128]
        dep_send[o, 8:16] = summed[8 * o : 8 * o + 8, 128:256]

    for y in range(4):
        away, copy = deposit_copy(y)
        pl.when(away)(copy.start)

    def group(lane):
        return ((lane + 4) & 127) // 16

    def pack_ends(c, x_list, first, count, keep):
        size = (count, 128)
        where = group(lanes(size))
        for i in range(5):
            found = [x for x in x_list if spot(x)[0] == i]
            packed = ends[c, i, first : first + count] if keep else jnp.zeros(size, F32)
            for x in found:
                turned = pltpu.roll(planes[c, x + 4, first : first + count], 16 * spot(x)[1] + 4, axis=1)
                packed = jnp.where(where == spot(x)[1], turned, packed)
            if found or not keep:
                ends[c, i, first : first + count] = packed

    inside = range(32)
    outside = (-4, -3, -2, -1, 32, 33, 34, 35)

    def pack_own(c, _):
        pack_ends(c, inside, 0, 32, False)
        return 0

    lax.fori_loop(0, 4, pack_own, 0)
    quarter = lanes(shape) % 16 // 4
    for i in range(5):
        up, down = jnp.zeros(shape, F32), jnp.zeros(shape, F32)
        for c in range(4):
            both = ends[c, i, 0:32]
            up = jnp.where(quarter == c, pltpu.roll(both, 4 * c, axis=1) if c else both, up)
            down = jnp.where(quarter == c, pltpu.roll(both, (4 * c - 4) % 128, axis=1) if c != 1 else both, down)
        slab_up[i] = up
        slab_down[i] = down

    for pair in range(3):
        a, b = 2 * pair, min(2 * pair + 1, 4)
        edge_send[0, pair] = rows_down(slab_up[a, 0:8], slab_up[b, 0:8])
        edge_send[1, pair] = rows_up(slab_up[a, 24:32], slab_up[b, 24:32])
        edge_send[2, pair] = rows_down(slab_down[a, 0:8], slab_down[b, 0:8])
        edge_send[3, pair] = rows_up(slab_down[a, 24:32], slab_down[b, 24:32])

    for message in edges + z_far:
        message.start()

    def clear(step, *refs):
        @pl.when(jnp.logical_not(there(step)))
        def _():
            for ref in refs:
                ref[...] = jnp.zeros(ref.shape, F32)

    clear(north, strip_from_above)
    clear(south, strip_from_below)
    clear((0, 0, -1), slab_below.at[:, 0:32])
    clear((0, 0, 1), slab_above.at[:, 0:32])
    for k, message_step in enumerate(((0, -1, 1), (0, 1, 1), (0, -1, -1), (0, 1, -1))):
        clear(back(message_step), edge_recv.at[k])
    clear(west, planes.at[:, 0:4, 0:32], planes.at[:, 1:4, 32:40], cross_recv.at[0])
    clear(east, planes.at[:, 36:40, 0:32], planes.at[:, 36:39, 32:40], cross_recv.at[1])
    planes[:, 0, 32:40] = jnp.zeros((4, 8, 128), F32)
    planes[:, 39, 32:40] = jnp.zeros((4, 8, 128), F32)

    for message in y_far:
        message.wait_recv()

    def merged(from_above, from_below):
        a = jnp.where(top, from_above, from_below)
        b = pltpu.roll(jnp.where(top, from_below, from_above), 4, axis=0)
        return a, b

    def merge_y(k, _):
        for x in (8 * k + n for n in range(8)):
            for pair in range(2):
                a, b = merged(strip_from_above[pair, x], strip_from_below[pair, x])
                planes[2 * pair, x + 4, 32:40] = a
                planes[2 * pair + 1, x + 4, 32:40] = b
        return 0

    lax.fori_loop(0, 4, merge_y, 0)
    x_rows = [
        Message(12, east, planes.at[:, 33:36, 32:40], planes.at[:, 1:4, 32:40]),
        Message(13, west, planes.at[:, 4:7, 32:40], planes.at[:, 36:39, 32:40]),
    ]
    for message in x_rows:
        message.start()

    def spread(c, X, j):
        return planes[c, X, pl.ds(j, 8, stride=5), :]

    def beside_y(read, c, X, j):
        above = read(c, X, j + 1) if j < 4 else pltpu.roll(read(c, X, 0), 7, axis=0)
        below = read(c, X, j - 1) if j > 0 else pltpu.roll(read(c, X, 4), 1, axis=0)
        return above, below

    def weigh(X):
        for j in range(5):
            centre = spread(3, X, j)
            above, below = beside_y(spread, 3, X, j)
            sides = (
                spread(3, X + 1, j), spread(3, X - 1, j), above, below,
                pltpu.roll(centre, 127, axis=1), pltpu.roll(centre, 1, axis=1),
            )
            weight = 6.0 * centre
            for side in sides:
                weight = weight + side
            inverse = jnp.where(centre > 0.0, 1.0 / weight, 0.0)
            for n, side in enumerate(sides):
                weights[n, X, j] = (centre + side) * inverse

    def reader(field):
        return lambda c, X, j: field[c, X, j]

    def to_field(field):
        def write(c, X, j, value):
            field[c, X, j] = value

        return write

    def to_result(c, X, j, value):
        result[c, X - 4, pl.ds(j, 8, stride=5), :] = value

    def relax(read, write, X):
        for j in range(5):
            w = [weights[n, X, j] for n in range(6)]
            for c in range(3):
                centre = read(c, X, j)
                above, below = beside_y(read, c, X, j)
                total = w[0] * read(c, X + 1, j) + w[1] * read(c, X - 1, j)
                total = total + (w[2] * above + w[3] * below)
                total = total + (w[4] * pltpu.roll(centre, 127, axis=1) + w[5] * pltpu.roll(centre, 1, axis=1))
                write(c, X, j, total)

    def span(body, start, stop, many):
        def step(k, _):
            first = jnp.minimum(start + k * many, stop - many)
            for n in range(many):
                body(first + n)
            return 0

        lax.fori_loop(0, -(-(stop - start) // many), step, 0)

    stages = (
        (spread, to_field(field_a)), (reader(field_a), to_field(field_b)),
        (reader(field_b), to_field(field_a)), (reader(field_a), to_result),
    )
    MANY = (10, 14, 13, 12)
    span(weigh, 5, 35, 10)
    def interior(sweep):
        read, write = stages[sweep]
        span(lambda X: relax(read, write, X), 5 + sweep, 35 - sweep, MANY[sweep])

    interior(0)

    for message in z_far + edges:
        message.wait_recv()
    for pair in range(3):
        a, b = merged(edge_recv[0, pair], edge_recv[1, pair])
        slab_below[2 * pair, 32:40] = a
        if pair < 2:
            slab_below[2 * pair + 1, 32:40] = b
        a, b = merged(edge_recv[2, pair], edge_recv[3, pair])
        slab_above[2 * pair, 32:40] = a
        if pair < 2:
            slab_above[2 * pair + 1, 32:40] = b
    tall = (EXT, 128)
    sixteen = lanes(tall) // 16
    far_x = ((28, 29, 30, 31), (0, 1, 2, 3))
    halo_x = ((-4, -3, -2, -1), (32, 33, 34, 35))
    for d in range(2):
        cross = jnp.zeros(tall, F32)
        for k, x in enumerate(far_x[d]):
            i, g = spot(x)
            cross = jnp.where(sixteen == k, pltpu.roll(slab_below[i], (16 * (k - g)) % 128, axis=1), cross)
            cross = jnp.where(sixteen == 4 + k, pltpu.roll(slab_above[i], (16 * (4 + k - g)) % 128, axis=1), cross)
        cross_send[d] = cross
    x_cross = [
        Message(14, east, cross_send.at[0], cross_recv.at[0]),
        Message(15, west, cross_send.at[1], cross_recv.at[1]),
    ]
    for message in x_cross:
        message.start()

    @pl.when(on_wall)
    def _():
        everyone = pltpu.make_async_remote_copy(
            src_ref=dep_recv, dst_ref=dep_recv, send_sem=send_sem.at[24], recv_sem=dep_sem.at[0],
            device_id=(gx, 0, 0), device_id_type=MESH,
        )
        everyone.wait_recv()
        total = dep_send[gy]
        for k in range(31):
            total = total + dep_recv[k]
        face = total[0:8] / (1.0 + total[8:16])
        wide = (8, 640)
        at = lanes(wide)
        which = 5 * (at % 128 // 16) + at // 128 - 4
        acc = jnp.zeros((96, 640), F32)
        for q in range(4):
            mask = mask_v[pl.ds(q, 8, stride=4), :].astype(F32)
            part = face[:, 32 * q : 32 * q + 32] * (-mask)
            values = jnp.concatenate([part * dir_v[c, pl.ds(q, 8, stride=4), :] for c in range(3)], axis=1)
            pick = ((at % 16 == 3) & (which == 4 * rows(wide) + q)).astype(F32)
            acc = acc + lax.dot_general(
                values, pick, (((0,), (0,)), ((), ())), precision=lax.Precision.HIGHEST, preferred_element_type=F32
            )
        short = (32, 128)
        eighth = lanes(short) // 16
        for c in range(3):
            own = [acc[32 * c : 32 * c + 32, 128 * i : 128 * i + 128] for i in range(5)]
            for i in range(5):
                ghost[i, c] = own[i]
            for d in range(2):
                cross = jnp.zeros(short, F32)
                for k, x in enumerate(far_x[d]):
                    i, g = spot(x)
                    cross = jnp.where(eighth == k, pltpu.roll(own[i], (16 * (k - g)) % 128, axis=1), cross)
                ghost_cross[d, c] = cross

    g_side = [
        Message(16, north, ghost.at[:, :, 24:32], ghost_side.at[0], True),
        Message(17, south, ghost.at[:, :, 0:8], ghost_side.at[1], True),
    ]
    g_face = [
        Message(18, east, ghost_cross.at[0], ghost_face.at[0], True),
        Message(19, west, ghost_cross.at[1], ghost_face.at[1], True),
    ]
    g_corner = [
        Message(20, (1, 1, 0), ghost_cross.at[0, :, 24:32], ghost_corner.at[0], True),
        Message(21, (1, -1, 0), ghost_cross.at[0, :, 0:8], ghost_corner.at[1], True),
        Message(22, (-1, 1, 0), ghost_cross.at[1, :, 24:32], ghost_corner.at[2], True),
        Message(23, (-1, -1, 0), ghost_cross.at[1, :, 0:8], ghost_corner.at[3], True),
    ]
    g_all = g_side + g_face + g_corner
    for message in g_all:
        message.start()
    clear(south, ghost_side.at[0])
    clear(north, ghost_side.at[1])
    clear(west, ghost_face.at[0])
    clear(east, ghost_face.at[1])
    for k, step in enumerate(((1, 1, 0), (1, -1, 0), (-1, 1, 0), (-1, -1, 0))):
        clear(back(step), ghost_corner.at[k])

    for sweep in (1, 2, 3):
        interior(sweep)


    for message in x_far + x_rows:
        message.wait_recv()
    def both_ends(body, left, right):
        def step(k, _):
            start = jnp.where(k == 0, left, right)
            for n in range(4):
                body(start + n)
            return 0

        lax.fori_loop(0, 2, step, 0)

    both_ends(weigh, 1, 35)
    for sweep, (read, write) in enumerate(stages):
        both_ends(lambda X, read=read, write=write: relax(read, write, X), 1 + sweep, 35 - sweep)

    for message in x_cross:
        message.wait_recv()

    def pack_rest(c, _):
        pack_ends(c, inside, 32, 8, False)
        pack_ends(c, outside, 0, 32, True)
        pack_ends(c, outside, 32, 8, True)
        return 0

    lax.fori_loop(0, 4, pack_rest, 0)
    for d in range(2):
        for k, x in enumerate(halo_x[d]):
            i, g = spot(x)
            from_below = pltpu.roll(cross_recv[d], (16 * (g - k)) % 128, axis=1)
            from_above = pltpu.roll(cross_recv[d], (16 * (g - 4 - k)) % 128, axis=1)
            slab_below[i] = jnp.where(sixteen == g, from_below, slab_below[i])
            slab_above[i] = jnp.where(sixteen == g, from_above, slab_above[i])
    place = lanes(tall) % 16
    for c in range(4):
        for i in range(5):
            under = pltpu.roll(slab_below[i], (128 - 4 * c) % 128, axis=1) if c else slab_below[i]
            over = pltpu.roll(slab_above[i], (4 - 4 * c) % 128, axis=1) if c != 1 else slab_above[i]
            halos[c, i] = jnp.where(place < 4, under, jnp.where(place < 8, over, 0.0))

    tile_place = tile_lane % 16
    low_end = (tile_place >= 4) & (tile_place < 12)
    high_end = (tile_place >= 12) | (tile_place < 4)

    def side_raw(step, _):
        c, i = lax.div(step, 5), lax.rem(step, 5)
        for j in range(5):
            own = ends[c, i, pl.ds(j, 8, stride=5), :]
            halo = halos[c, i, pl.ds(j, 8, stride=5), :]
            low = jnp.where(low_end, own, halo)
            side_a[0, c, i, j] = low
            side_a[1, c, i, j] = jnp.where(high_end, own, halo)
        return 0

    lax.fori_loop(0, 20, side_raw, 0)
    def side_sides(field, e, c, i, j):
        here = field[e, c, i, j]
        return (
            field[e, c, i + 1, j] if i < 4 else pltpu.roll(field[e, c, 0, j], 112, axis=1),
            field[e, c, i - 1, j] if i > 0 else pltpu.roll(field[e, c, 4, j], 16, axis=1),
            field[e, c, i, j + 1] if j < 4 else pltpu.roll(field[e, c, i, 0], 7, axis=0),
            field[e, c, i, j - 1] if j > 0 else pltpu.roll(field[e, c, i, 4], 1, axis=0),
            pltpu.roll(here, 127, axis=1),
            pltpu.roll(here, 1, axis=1),
        )

    def side_weigh(e, _):
        for i in range(5):
            for j in range(5):
                centre = side_a[e, 3, i, j]
                sides = side_sides(side_a, e, 3, i, j)
                weight = 6.0 * centre
                for side in sides:
                    weight = weight + side
                inverse = jnp.where(centre > 0.0, 1.0 / weight, 0.0)
                for n, side in enumerate(sides):
                    side_weights[n, e, i, j] = (centre + side) * inverse
        return 0

    lax.fori_loop(0, 2, side_weigh, 0)
    def side_sweeps(e):
        for sweep in range(SWEEPS):
            src, dst = (side_a, side_b) if sweep % 2 == 0 else (side_b, side_a)

            for c in range(3):
                for i in range(5):
                    for j in range(5):
                        sides = side_sides(src, e, c, i, j)
                        total = side_weights[0, e, i, j] * sides[0]
                        for n in range(1, 6):
                            total = total + side_weights[n, e, i, j] * sides[n]
                        dst[e, c, i, j] = total + side_source[c, i, j] if e == 0 else total

    side_sweeps(1)

    side_source[...] = jnp.zeros(side_source.shape, F32)

    @pl.when(on_wall)
    def _():
        for message in g_all:
            message.wait_recv()
        eighth = lanes((32, 128)) // 16
        eighth_tile = tile_lane // 16
        for c in range(3):
            whole = [ghost[i, c] for i in range(5)]
            rest = [jnp.where(top, ghost_side[1, i, c], ghost_side[0, i, c]) for i in range(5)]
            for d in range(2):
                face = ghost_face[d, c]
                corner = jnp.where(top, ghost_corner[2 * d + 1, c], ghost_corner[2 * d, c])
                for k, x in enumerate(halo_x[d]):
                    i, g = spot(x)
                    whole[i] = jnp.where(eighth == g, pltpu.roll(face, (16 * (g - k)) % 128, axis=1), whole[i])
                    rest[i] = jnp.where(eighth_tile == g, pltpu.roll(corner, (16 * (g - k)) % 128, axis=1), rest[i])
            for i in range(5):
                ghost_all[c, i, 0:32] = whole[i]
                ghost_all[c, i, 32:40] = rest[i]
        for c in range(3):
            for i in range(5):
                for j in range(5):
                    side_source[c, i, j] = ghost_all[c, i, pl.ds(j, 8, stride=5), :]

    for c in range(3):
        for i in range(5):
            for j in range(5):
                side_a[0, c, i, j] = side_a[0, c, i, j] + side_source[c, i, j]

    side_sweeps(0)

    for c in range(3):
        for i in range(5):
            for j in range(5):
                both = jnp.where(tile_place < 4, side_a[1, c, i, j], side_a[0, c, i, j])
                ends[c, i, pl.ds(j, 8, stride=5), :] = both
    edge_rows = (lanes(shape) < 4) | (lanes(shape) >= 124)

    def put_back(c, _):
        for x in inside:
            i, g = spot(x)
            turned = pltpu.roll(ends[c, i, 0:32], 128 - 16 * g - 4, axis=1)
            disp_out[c, x] = jnp.where(edge_rows, turned, result[c, x, 0:32])
        return 0

    lax.fori_loop(0, 3, put_back, 0)

    for message in x_far + y_far + z_far + edges + x_rows + x_cross + g_all:
        message.wait_send()
    for y in range(4):
        away, copy = deposit_copy(y)
        pl.when(away)(copy.wait_send)


def local(
    recovery_temp, film_coeff, emissivity, char_density, back_temp, stencil_frac,
    wall_owner, stencil_start, live_count, wall_mask, wall_dir, stiffness, start_disp,
):
    vmem = pl.BlockSpec(memory_space=pltpu.VMEM)
    hbm = pl.BlockSpec(memory_space=pltpu.HBM)
    def f32(*shape):
        return pltpu.VMEM(shape, F32)

    def i32(*shape):
        return pltpu.VMEM(shape, jnp.int32)

    scratch = [f32(32, 128)] * 6 + [i32(1, 32)] * 3 + [i32(32, 32), f32(3, 32, 32)]
    scratch += [
        f32(4, EXT, EXT, 128),
        f32(2, 32, 8, 128),
        f32(2, 32, 8, 128),
        f32(2, 32, 8, 128),
        f32(2, 32, 8, 128),
        f32(5, 32, 128),
        f32(5, 32, 128),
        f32(5, EXT, 128),
        f32(5, EXT, 128),
        f32(4, 3, 8, 128),
        f32(4, 3, 8, 128),
        f32(2, EXT, 128),
        f32(2, EXT, 128),
        f32(4, 5, EXT, 128),
        f32(4, 5, EXT, 128),
        f32(6, EXT, 5, 8, 128),
        f32(3, EXT, 5, 8, 128),
        f32(3, EXT, 5, 8, 128),
        f32(3, 32, EXT, 128),
        f32(6, 2, 5, 5, 8, 128),
        f32(2, 4, 5, 5, 8, 128),
        f32(2, 3, 5, 5, 8, 128),
        f32(3, 5, 5, 8, 128),
        f32(4, 16, 128),
        f32(31, 16, 128),
        f32(5, 3, 32, 128),
        f32(2, 3, 32, 128),
        f32(2, 5, 3, 8, 128),
        f32(2, 3, 32, 128),
        f32(4, 3, 8, 128),
        f32(3, 5, EXT, 128),
    ]
    return pl.pallas_call(
        kernel,
        out_shape=(pltpu.VMEM(back_temp.shape, F32), pltpu.VMEM(start_disp.shape, F32)),
        in_specs=[hbm] * 13,
        out_specs=(vmem, vmem),
        scratch_shapes=scratch
        + [
            pltpu.SemaphoreType.DMA((19,)),
            pltpu.SemaphoreType.DMA((28,)),
            pltpu.SemaphoreType.DMA((24,)),
            pltpu.SemaphoreType.DMA((1,)),
        ],
        compiler_params=pltpu.CompilerParams(collective_id=0, has_side_effects=True, vmem_limit_bytes=32 << 20),
    )(
        *(
            pltpu.with_memory_space_constraint(x, pltpu.HBM)
            for x in (
                recovery_temp, film_coeff, emissivity, char_density, back_temp, stencil_frac,
                wall_owner.reshape(1, 32), stencil_start.reshape(1, 32), live_count.reshape(1, 32),
                wall_mask, wall_dir, stiffness, start_disp,
            )
        )
    )


def solution(mesh):
    tiles = P(("gx", "gy", "gz"), None)
    flat = P(("gx", "gy", "gz"))
    in_specs = (tiles,) * 7 + (flat, flat, P("gx", "gy"), P(None, "gx", "gy"), P("gx", "gy", "gz"), P(None, "gx", "gy", "gz"))
    out_specs = (tiles, P(None, "gx", "gy", "gz"))
    return jax.shard_map(local, mesh=mesh, in_specs=in_specs, out_specs=out_specs, check_vma=False)
```

```python
import jax
import jax.numpy as jnp
from jax import lax
from jax.experimental import pallas as pl
from jax.experimental.pallas import tpu as pltpu
from jax.sharding import PartitionSpec as P

NEWTON = 6
SWEEPS = 4
MESH = pl.DeviceIdType.MESH
F32 = jnp.float32
SIZES = {"gx": 8, "gy": 4, "gz": 8}
EXT = 40

arrhenius_scale = 0.5
activation = 3.0
blowing = 0.5
heat_release = 0.3
radiation = 0.05
conduction = 0.5
time_step = 1.5


def ablation_rate(surface):
    return arrhenius_scale * jnp.exp(activation * (1.0 - 1.0 / surface))


def balance_step(surface, recovery_temp, film_coeff, emissivity, back_temp):
    ablate = ablation_rate(surface)
    film = film_coeff * film_coeff / (film_coeff + blowing * ablate)
    cubed = surface * surface * surface
    imbalance = (
        film * (recovery_temp - surface)
        + heat_release * ablate
        - radiation * emissivity * (cubed * surface)
        - conduction * (surface - back_temp)
    )
    slope = film + 4.0 * radiation * emissivity * cubed + conduction
    return surface + imbalance / slope


def lanes(shape):
    return lax.broadcasted_iota(jnp.int32, shape, len(shape) - 1)


def rows(shape):
    return lax.broadcasted_iota(jnp.int32, shape, len(shape) - 2)


def spot(x):
    return (x + 4) % 5, (x + 4) // 5


def kernel(
    recovery_temp, film_coeff, emissivity, char_density, back_temp, stencil_frac,
    wall_owner, stencil_start, live_count, wall_mask, wall_dir, stiffness, start_disp,
    surface_out, disp_out,
    recovery_v, film_v, emissivity_v, char_v, back_v, frac_v, owner_v, start_v, live_v, mask_v, dir_v,
    planes, strip_up, strip_down, strip_from_below, strip_from_above,
    slab_up, slab_down, slab_below, slab_above, edge_send, edge_recv, cross_send, cross_recv,
    ends, halos, weights, field_a, field_b, result,
    side_weights, side_a, side_b, side_source,
    dep_send, dep_recv, ghost, ghost_cross, ghost_side, ghost_face, ghost_corner, ghost_all,
    local_sem, send_sem, recv_sem, dep_sem,
):
    gx, gy, gz = (lax.axis_index(a) for a in ("gx", "gy", "gz"))
    position = (gx, gy, gz)
    limits = (SIZES["gx"], SIZES["gy"], SIZES["gz"])

    def there(step):
        found = None
        for p, d, n in zip(position, step, limits):
            if d != 0:
                ok = (p + d >= 0) & (p + d < n)
                found = ok if found is None else found & ok
        return found

    def target(step):
        return tuple(p + d for p, d in zip(position, step))

    def back(step):
        return tuple(-d for d in step)

    on_wall = gz == 0

    class Message:
        def __init__(self, channel, step, src, dst, walls=False):
            self.to, self.origin = there(step), there(back(step))
            if walls:
                self.to, self.origin = self.to & on_wall, self.origin & on_wall
            self.copy = pltpu.make_async_remote_copy(
                src_ref=src, dst_ref=dst, send_sem=send_sem.at[channel], recv_sem=recv_sem.at[channel],
                device_id=target(step), device_id_type=MESH,
            )

        def start(self):
            pl.when(self.to)(self.copy.start)

        def wait_recv(self):
            pl.when(self.origin)(self.copy.wait_recv)

        def wait_send(self):
            pl.when(self.to)(self.copy.wait_send)

    small = [
        pltpu.make_async_copy(src, dst, local_sem.at[8 + k])
        for k, (src, dst) in enumerate((
            (recovery_temp, recovery_v), (film_coeff, film_v), (emissivity, emissivity_v), (char_density, char_v),
            (back_temp, back_v), (stencil_frac, frac_v), (wall_owner, owner_v), (stencil_start, start_v),
            (live_count, live_v), (wall_mask, mask_v), (wall_dir, dir_v),
        ))
    ]
    for copy in small:
        copy.start()
    load_u = pltpu.make_async_copy(start_disp, planes.at[0:3, 4:36, 0:32], local_sem.at[0])
    load_k = pltpu.make_async_copy(stiffness, planes.at[3, 4:36, 0:32], local_sem.at[1])
    load_u.start()
    load_k.start()

    barrier = pltpu.get_barrier_semaphore()
    near = [(1, 0, 0), (-1, 0, 0), (0, 1, 0), (0, -1, 0), (0, 0, 1), (0, 0, -1)]
    near += [(0, a, b) for a in (1, -1) for b in (1, -1)]
    corners = [(a, b, 0) for a in (1, -1) for b in (1, -1)]
    expected = jnp.where(on_wall, 3, 4)

    def greet(step, ok):
        pl.when(ok)(lambda: pl.semaphore_signal(barrier, inc=1, device_id=target(step), device_id_type=MESH))
        return ok.astype(jnp.int32)

    for step in near:
        expected = expected + greet(step, there(step))
    for step in corners:
        expected = expected + greet(step, there(step) & on_wall)
    rank = gy * limits[2] + gz
    for y in range(limits[1]):
        for z in range(limits[2]):
            pl.when(on_wall & (rank != y * limits[2] + z))(
                lambda y=y, z=z: pl.semaphore_signal(barrier, inc=1, device_id=(gx, y, z), device_id_type=MESH)
            )

    tile = (8, 128)
    top = rows(tile) < 4
    tile_lane = lanes(tile)
    load_u.wait()
    load_k.wait()

    def rows_down(a, b):
        return jnp.where(top, a, pltpu.roll(b, 4, axis=0))

    def rows_up(a, b):
        return jnp.where(top, pltpu.roll(b, 4, axis=0), a)

    def pack_y(k, _):
        for x in (8 * k + n for n in range(8)):
            for pair in range(2):
                a, b = 2 * pair, 2 * pair + 1
                strip_down[pair, x] = rows_down(planes[a, x + 4, 0:8], planes[b, x + 4, 0:8])
                strip_up[pair, x] = rows_up(planes[a, x + 4, 24:32], planes[b, x + 4, 24:32])
        return 0

    lax.fori_loop(0, 4, pack_y, 0)
    east, west, north, south = (1, 0, 0), (-1, 0, 0), (0, 1, 0), (0, -1, 0)
    x_far = [
        Message(0, east, start_disp.at[:, 28:32], planes.at[0:3, 0:4, 0:32]),
        Message(1, east, stiffness.at[28:32], planes.at[3, 0:4, 0:32]),
        Message(2, west, start_disp.at[:, 0:4], planes.at[0:3, 36:40, 0:32]),
        Message(3, west, stiffness.at[0:4], planes.at[3, 36:40, 0:32]),
    ]
    y_far = [Message(4, north, strip_up, strip_from_below), Message(5, south, strip_down, strip_from_above)]
    z_far = [
        Message(6, (0, 0, 1), slab_up, slab_below.at[:, 0:32]),
        Message(7, (0, 0, -1), slab_down, slab_above.at[:, 0:32]),
    ]
    edges = [
        Message(8, (0, -1, 1), edge_send.at[0], edge_recv.at[0]),
        Message(9, (0, 1, 1), edge_send.at[1], edge_recv.at[1]),
        Message(10, (0, -1, -1), edge_send.at[2], edge_recv.at[2]),
        Message(11, (0, 1, -1), edge_send.at[3], edge_recv.at[3]),
    ]

    pl.semaphore_wait(barrier, expected)

    def deposit_copy(y):
        ahead = lax.rem(rank - y * limits[2] + 32, 32)
        slot = jnp.maximum(ahead - 1, 0)
        copy = pltpu.make_async_remote_copy(
            src_ref=dep_send.at[y], dst_ref=dep_recv.at[slot], send_sem=send_sem.at[24 + y], recv_sem=dep_sem.at[0],
            device_id=(gx, y, 0), device_id_type=MESH,
        )
        return ahead != 0, copy

    for message in y_far + x_far:
        message.start()

    for copy in small:
        copy.wait()
    back_t = back_v[...]
    surface = back_t
    for _ in range(NEWTON):
        surface = balance_step(surface, recovery_v[...], film_v[...], emissivity_v[...], back_t)
    surface_out[...] = surface
    recession = time_step * ablation_rate(surface) / char_v[...]
    shape = (32, 128)
    lane = lanes(shape)
    square = (32, 32)
    diagonal = rows(square) == lanes(square)

    def column(row):
        spread = jnp.broadcast_to(row.astype(F32), square)
        return jnp.broadcast_to(jnp.sum(jnp.where(diagonal, spread, 0.0), axis=1, keepdims=True), shape)

    starts = start_v[...]
    shift = column(starts & 127)
    live = lane.astype(F32) < column(live_v[...])
    upper = jnp.where(live, frac_v[...], 0.0)
    lower = jnp.where(live, 1.0 - frac_v[...], 0.0)
    shift = shift.astype(jnp.int32)
    first, second = [], []
    for low, high in ((lower * recession, upper * recession), (lower, upper)):
        moved = pltpu.roll(high, 1, axis=1)
        spread = low + jnp.where(lane >= 1, moved, 0.0)
        last = jnp.broadcast_to(moved[:, 0:1], shape)
        for bit in range(7):
            spread = jnp.where(((shift >> bit) & 1) == 1, pltpu.roll(spread, 1 << bit, axis=1), spread)
        first.append(jnp.where(lane >= shift, spread, 0.0))
        second.append(jnp.where(lane < shift, spread, jnp.where(lane == shift, last, 0.0)))
    face_row = owner_v[...] * 8
    row_a = jnp.broadcast_to(face_row + (starts >> 7), square)
    row_b = jnp.broadcast_to(face_row + (((starts >> 7) + 1) & 7), square)

    def gathered(row, terms):
        pick = (rows(square) == row).astype(F32)
        return jnp.dot(pick, terms, precision=lax.Precision.HIGHEST, preferred_element_type=F32)

    summed = gathered(row_a, jnp.concatenate(first, axis=1)) + gathered(row_b, jnp.concatenate(second, axis=1))
    for o in range(4):
        dep_send[o, 0:8] = summed[8 * o : 8 * o + 8, 0:128]
        dep_send[o, 8:16] = summed[8 * o : 8 * o + 8, 128:256]

    for y in range(4):
        away, copy = deposit_copy(y)
        pl.when(away)(copy.start)

    def group(lane):
        return ((lane + 4) & 127) // 16

    def pack_ends(c, x_list, first, count, keep):
        size = (count, 128)
        where = group(lanes(size))
        for i in range(5):
            found = [x for x in x_list if spot(x)[0] == i]
            packed = ends[c, i, first : first + count] if keep else jnp.zeros(size, F32)
            for x in found:
                turned = pltpu.roll(planes[c, x + 4, first : first + count], 16 * spot(x)[1] + 4, axis=1)
                packed = jnp.where(where == spot(x)[1], turned, packed)
            if found or not keep:
                ends[c, i, first : first + count] = packed

    inside = range(32)
    outside = (-4, -3, -2, -1, 32, 33, 34, 35)

    def pack_own(c, _):
        pack_ends(c, inside, 0, 32, False)
        return 0

    lax.fori_loop(0, 4, pack_own, 0)
    quarter = lanes(shape) % 16 // 4
    for i in range(5):
        up, down = jnp.zeros(shape, F32), jnp.zeros(shape, F32)
        for c in range(4):
            both = ends[c, i, 0:32]
            up = jnp.where(quarter == c, pltpu.roll(both, 4 * c, axis=1) if c else both, up)
            down = jnp.where(quarter == c, pltpu.roll(both, (4 * c - 4) % 128, axis=1) if c != 1 else both, down)
        slab_up[i] = up
        slab_down[i] = down

    for pair in range(3):
        a, b = 2 * pair, min(2 * pair + 1, 4)
        edge_send[0, pair] = rows_down(slab_up[a, 0:8], slab_up[b, 0:8])
        edge_send[1, pair] = rows_up(slab_up[a, 24:32], slab_up[b, 24:32])
        edge_send[2, pair] = rows_down(slab_down[a, 0:8], slab_down[b, 0:8])
        edge_send[3, pair] = rows_up(slab_down[a, 24:32], slab_down[b, 24:32])

    for message in edges + z_far:
        message.start()

    def clear(step, *refs):
        @pl.when(jnp.logical_not(there(step)))
        def _():
            for ref in refs:
                ref[...] = jnp.zeros(ref.shape, F32)

    clear(north, strip_from_above)
    clear(south, strip_from_below)
    clear((0, 0, -1), slab_below.at[:, 0:32])
    clear((0, 0, 1), slab_above.at[:, 0:32])
    for k, message_step in enumerate(((0, -1, 1), (0, 1, 1), (0, -1, -1), (0, 1, -1))):
        clear(back(message_step), edge_recv.at[k])
    clear(west, planes.at[:, 0:4, 0:32], planes.at[:, 1:4, 32:40], cross_recv.at[0])
    clear(east, planes.at[:, 36:40, 0:32], planes.at[:, 36:39, 32:40], cross_recv.at[1])
    planes[:, 0, 32:40] = jnp.zeros((4, 8, 128), F32)
    planes[:, 39, 32:40] = jnp.zeros((4, 8, 128), F32)

    for message in y_far:
        message.wait_recv()

    def merged(from_above, from_below):
        a = jnp.where(top, from_above, from_below)
        b = pltpu.roll(jnp.where(top, from_below, from_above), 4, axis=0)
        return a, b

    def merge_y(k, _):
        for x in (8 * k + n for n in range(8)):
            for pair in range(2):
                a, b = merged(strip_from_above[pair, x], strip_from_below[pair, x])
                planes[2 * pair, x + 4, 32:40] = a
                planes[2 * pair + 1, x + 4, 32:40] = b
        return 0

    lax.fori_loop(0, 4, merge_y, 0)
    x_rows = [
        Message(12, east, planes.at[:, 33:36, 32:40], planes.at[:, 1:4, 32:40]),
        Message(13, west, planes.at[:, 4:7, 32:40], planes.at[:, 36:39, 32:40]),
    ]
    for message in x_rows:
        message.start()

    def spread(c, X, j):
        return planes[c, X, pl.ds(j, 8, stride=5), :]

    def beside_y(read, c, X, j):
        above = read(c, X, j + 1) if j < 4 else pltpu.roll(read(c, X, 0), 7, axis=0)
        below = read(c, X, j - 1) if j > 0 else pltpu.roll(read(c, X, 4), 1, axis=0)
        return above, below

    def weigh(X):
        for j in range(5):
            centre = spread(3, X, j)
            above, below = beside_y(spread, 3, X, j)
            sides = (
                spread(3, X + 1, j), spread(3, X - 1, j), above, below,
                pltpu.roll(centre, 127, axis=1), pltpu.roll(centre, 1, axis=1),
            )
            weight = 6.0 * centre
            for side in sides:
                weight = weight + side
            inverse = jnp.where(centre > 0.0, 1.0 / weight, 0.0)
            for n, side in enumerate(sides):
                weights[n, X, j] = (centre + side) * inverse

    def reader(field):
        return lambda c, X, j: field[c, X, j]

    def to_field(field):
        def write(c, X, j, value):
            field[c, X, j] = value

        return write

    def to_result(c, X, j, value):
        result[c, X - 4, pl.ds(j, 8, stride=5), :] = value

    def relax(read, write, X):
        for j in range(5):
            w = [weights[n, X, j] for n in range(6)]
            for c in range(3):
                centre = read(c, X, j)
                above, below = beside_y(read, c, X, j)
                total = w[0] * read(c, X + 1, j) + w[1] * read(c, X - 1, j)
                total = total + (w[2] * above + w[3] * below)
                total = total + (w[4] * pltpu.roll(centre, 127, axis=1) + w[5] * pltpu.roll(centre, 1, axis=1))
                write(c, X, j, total)

    def span(body, start, stop, many):
        def step(k, _):
            first = jnp.minimum(start + k * many, stop - many)
            for n in range(many):
                body(first + n)
            return 0

        lax.fori_loop(0, -(-(stop - start) // many), step, 0)

    stages = (
        (spread, to_field(field_a)), (reader(field_a), to_field(field_b)),
        (reader(field_b), to_field(field_a)), (reader(field_a), to_result),
    )
    MANY = (10, 14, 13, 12)
    span(weigh, 5, 35, 10)
    def interior(sweep):
        read, write = stages[sweep]
        span(lambda X: relax(read, write, X), 5 + sweep, 35 - sweep, MANY[sweep])

    interior(0)

    interior(1)
    interior(2)

    for message in z_far + edges:
        message.wait_recv()
    for pair in range(3):
        a, b = merged(edge_recv[0, pair], edge_recv[1, pair])
        slab_below[2 * pair, 32:40] = a
        if pair < 2:
            slab_below[2 * pair + 1, 32:40] = b
        a, b = merged(edge_recv[2, pair], edge_recv[3, pair])
        slab_above[2 * pair, 32:40] = a
        if pair < 2:
            slab_above[2 * pair + 1, 32:40] = b
    tall = (EXT, 128)
    sixteen = lanes(tall) // 16
    far_x = ((28, 29, 30, 31), (0, 1, 2, 3))
    halo_x = ((-4, -3, -2, -1), (32, 33, 34, 35))
    for d in range(2):
        cross = jnp.zeros(tall, F32)
        for k, x in enumerate(far_x[d]):
            i, g = spot(x)
            cross = jnp.where(sixteen == k, pltpu.roll(slab_below[i], (16 * (k - g)) % 128, axis=1), cross)
            cross = jnp.where(sixteen == 4 + k, pltpu.roll(slab_above[i], (16 * (4 + k - g)) % 128, axis=1), cross)
        cross_send[d] = cross
    x_cross = [
        Message(14, east, cross_send.at[0], cross_recv.at[0]),
        Message(15, west, cross_send.at[1], cross_recv.at[1]),
    ]
    for message in x_cross:
        message.start()

    @pl.when(on_wall)
    def _():
        everyone = pltpu.make_async_remote_copy(
            src_ref=dep_recv, dst_ref=dep_recv, send_sem=send_sem.at[24], recv_sem=dep_sem.at[0],
            device_id=(gx, 0, 0), device_id_type=MESH,
        )
        everyone.wait_recv()
        total = dep_send[gy]
        for k in range(31):
            total = total + dep_recv[k]
        face = total[0:8] / (1.0 + total[8:16])
        wide = (8, 640)
        at = lanes(wide)
        which = 5 * (at % 128 // 16) + at // 128 - 4
        acc = jnp.zeros((96, 640), F32)
        for q in range(4):
            mask = mask_v[pl.ds(q, 8, stride=4), :].astype(F32)
            part = face[:, 32 * q : 32 * q + 32] * (-mask)
            values = jnp.concatenate([part * dir_v[c, pl.ds(q, 8, stride=4), :] for c in range(3)], axis=1)
            pick = ((at % 16 == 3) & (which == 4 * rows(wide) + q)).astype(F32)
            acc = acc + lax.dot_general(
                values, pick, (((0,), (0,)), ((), ())), precision=lax.Precision.HIGHEST, preferred_element_type=F32
            )
        short = (32, 128)
        eighth = lanes(short) // 16
        for c in range(3):
            own = [acc[32 * c : 32 * c + 32, 128 * i : 128 * i + 128] for i in range(5)]
            for i in range(5):
                ghost[i, c] = own[i]
            for d in range(2):
                cross = jnp.zeros(short, F32)
                for k, x in enumerate(far_x[d]):
                    i, g = spot(x)
                    cross = jnp.where(eighth == k, pltpu.roll(own[i], (16 * (k - g)) % 128, axis=1), cross)
                ghost_cross[d, c] = cross

    g_side = [
        Message(16, north, ghost.at[:, :, 24:32], ghost_side.at[0], True),
        Message(17, south, ghost.at[:, :, 0:8], ghost_side.at[1], True),
    ]
    g_face = [
        Message(18, east, ghost_cross.at[0], ghost_face.at[0], True),
        Message(19, west, ghost_cross.at[1], ghost_face.at[1], True),
    ]
    g_corner = [
        Message(20, (1, 1, 0), ghost_cross.at[0, :, 24:32], ghost_corner.at[0], True),
        Message(21, (1, -1, 0), ghost_cross.at[0, :, 0:8], ghost_corner.at[1], True),
        Message(22, (-1, 1, 0), ghost_cross.at[1, :, 24:32], ghost_corner.at[2], True),
        Message(23, (-1, -1, 0), ghost_cross.at[1, :, 0:8], ghost_corner.at[3], True),
    ]
    g_all = g_side + g_face + g_corner
    for message in g_all:
        message.start()
    clear(south, ghost_side.at[0])
    clear(north, ghost_side.at[1])
    clear(west, ghost_face.at[0])
    clear(east, ghost_face.at[1])
    for k, step in enumerate(((1, 1, 0), (1, -1, 0), (-1, 1, 0), (-1, -1, 0))):
        clear(back(step), ghost_corner.at[k])

    for sweep in (3,):
        interior(sweep)


    for message in x_far + x_rows:
        message.wait_recv()
    def both_ends(body, left, right):
        def step(k, _):
            start = jnp.where(k == 0, left, right)
            for n in range(4):
                body(start + n)
            return 0

        lax.fori_loop(0, 2, step, 0)

    both_ends(weigh, 1, 35)
    for sweep, (read, write) in enumerate(stages):
        both_ends(lambda X, read=read, write=write: relax(read, write, X), 1 + sweep, 35 - sweep)

    for message in x_cross:
        message.wait_recv()

    def pack_rest(c, _):
        pack_ends(c, inside, 32, 8, False)
        pack_ends(c, outside, 0, 32, True)
        pack_ends(c, outside, 32, 8, True)
        return 0

    lax.fori_loop(0, 4, pack_rest, 0)
    for d in range(2):
        for k, x in enumerate(halo_x[d]):
            i, g = spot(x)
            from_below = pltpu.roll(cross_recv[d], (16 * (g - k)) % 128, axis=1)
            from_above = pltpu.roll(cross_recv[d], (16 * (g - 4 - k)) % 128, axis=1)
            slab_below[i] = jnp.where(sixteen == g, from_below, slab_below[i])
            slab_above[i] = jnp.where(sixteen == g, from_above, slab_above[i])
    place = lanes(tall) % 16
    for c in range(4):
        for i in range(5):
            under = pltpu.roll(slab_below[i], (128 - 4 * c) % 128, axis=1) if c else slab_below[i]
            over = pltpu.roll(slab_above[i], (4 - 4 * c) % 128, axis=1) if c != 1 else slab_above[i]
            halos[c, i] = jnp.where(place < 4, under, jnp.where(place < 8, over, 0.0))

    tile_place = tile_lane % 16
    low_end = (tile_place >= 4) & (tile_place < 12)
    high_end = (tile_place >= 12) | (tile_place < 4)

    def side_raw(step, _):
        c, i = lax.div(step, 5), lax.rem(step, 5)
        for j in range(5):
            own = ends[c, i, pl.ds(j, 8, stride=5), :]
            halo = halos[c, i, pl.ds(j, 8, stride=5), :]
            low = jnp.where(low_end, own, halo)
            side_a[0, c, i, j] = low
            side_a[1, c, i, j] = jnp.where(high_end, own, halo)
        return 0

    lax.fori_loop(0, 20, side_raw, 0)
    def side_sides(field, e, c, i, j):
        here = field[e, c, i, j]
        return (
            field[e, c, i + 1, j] if i < 4 else pltpu.roll(field[e, c, 0, j], 112, axis=1),
            field[e, c, i - 1, j] if i > 0 else pltpu.roll(field[e, c, 4, j], 16, axis=1),
            field[e, c, i, j + 1] if j < 4 else pltpu.roll(field[e, c, i, 0], 7, axis=0),
            field[e, c, i, j - 1] if j > 0 else pltpu.roll(field[e, c, i, 4], 1, axis=0),
            pltpu.roll(here, 127, axis=1),
            pltpu.roll(here, 1, axis=1),
        )

    def side_weigh(e, _):
        for i in range(5):
            for j in range(5):
                centre = side_a[e, 3, i, j]
                sides = side_sides(side_a, e, 3, i, j)
                weight = 6.0 * centre
                for side in sides:
                    weight = weight + side
                inverse = jnp.where(centre > 0.0, 1.0 / weight, 0.0)
                for n, side in enumerate(sides):
                    side_weights[n, e, i, j] = (centre + side) * inverse
        return 0

    lax.fori_loop(0, 2, side_weigh, 0)
    def side_sweeps(e):
        for sweep in range(SWEEPS):
            src, dst = (side_a, side_b) if sweep % 2 == 0 else (side_b, side_a)

            for c in range(3):
                for i in range(5):
                    for j in range(5):
                        sides = side_sides(src, e, c, i, j)
                        total = side_weights[0, e, i, j] * sides[0]
                        for n in range(1, 6):
                            total = total + side_weights[n, e, i, j] * sides[n]
                        dst[e, c, i, j] = total + side_source[c, i, j] if e == 0 else total

    side_sweeps(1)

    side_source[...] = jnp.zeros(side_source.shape, F32)

    @pl.when(on_wall)
    def _():
        for message in g_all:
            message.wait_recv()
        eighth = lanes((32, 128)) // 16
        eighth_tile = tile_lane // 16
        for c in range(3):
            whole = [ghost[i, c] for i in range(5)]
            rest = [jnp.where(top, ghost_side[1, i, c], ghost_side[0, i, c]) for i in range(5)]
            for d in range(2):
                face = ghost_face[d, c]
                corner = jnp.where(top, ghost_corner[2 * d + 1, c], ghost_corner[2 * d, c])
                for k, x in enumerate(halo_x[d]):
                    i, g = spot(x)
                    whole[i] = jnp.where(eighth == g, pltpu.roll(face, (16 * (g - k)) % 128, axis=1), whole[i])
                    rest[i] = jnp.where(eighth_tile == g, pltpu.roll(corner, (16 * (g - k)) % 128, axis=1), rest[i])
            for i in range(5):
                ghost_all[c, i, 0:32] = whole[i]
                ghost_all[c, i, 32:40] = rest[i]
        for c in range(3):
            for i in range(5):
                for j in range(5):
                    side_source[c, i, j] = ghost_all[c, i, pl.ds(j, 8, stride=5), :]

    for c in range(3):
        for i in range(5):
            for j in range(5):
                side_a[0, c, i, j] = side_a[0, c, i, j] + side_source[c, i, j]

    side_sweeps(0)

    for c in range(3):
        for i in range(5):
            for j in range(5):
                both = jnp.where(tile_place < 4, side_a[1, c, i, j], side_a[0, c, i, j])
                ends[c, i, pl.ds(j, 8, stride=5), :] = both
    edge_rows = (lanes(shape) < 4) | (lanes(shape) >= 124)

    def put_back(c, _):
        for x in inside:
            i, g = spot(x)
            turned = pltpu.roll(ends[c, i, 0:32], 128 - 16 * g - 4, axis=1)
            disp_out[c, x] = jnp.where(edge_rows, turned, result[c, x, 0:32])
        return 0

    lax.fori_loop(0, 3, put_back, 0)

    for message in x_far + y_far + z_far + edges + x_rows + x_cross + g_all:
        message.wait_send()
    for y in range(4):
        away, copy = deposit_copy(y)
        pl.when(away)(copy.wait_send)


def local(
    recovery_temp, film_coeff, emissivity, char_density, back_temp, stencil_frac,
    wall_owner, stencil_start, live_count, wall_mask, wall_dir, stiffness, start_disp,
):
    vmem = pl.BlockSpec(memory_space=pltpu.VMEM)
    hbm = pl.BlockSpec(memory_space=pltpu.HBM)
    def f32(*shape):
        return pltpu.VMEM(shape, F32)

    def i32(*shape):
        return pltpu.VMEM(shape, jnp.int32)

    scratch = [f32(32, 128)] * 6 + [i32(1, 32)] * 3 + [i32(32, 32), f32(3, 32, 32)]
    scratch += [
        f32(4, EXT, EXT, 128),
        f32(2, 32, 8, 128),
        f32(2, 32, 8, 128),
        f32(2, 32, 8, 128),
        f32(2, 32, 8, 128),
        f32(5, 32, 128),
        f32(5, 32, 128),
        f32(5, EXT, 128),
        f32(5, EXT, 128),
        f32(4, 3, 8, 128),
        f32(4, 3, 8, 128),
        f32(2, EXT, 128),
        f32(2, EXT, 128),
        f32(4, 5, EXT, 128),
        f32(4, 5, EXT, 128),
        f32(6, EXT, 5, 8, 128),
        f32(3, EXT, 5, 8, 128),
        f32(3, EXT, 5, 8, 128),
        f32(3, 32, EXT, 128),
        f32(6, 2, 5, 5, 8, 128),
        f32(2, 4, 5, 5, 8, 128),
        f32(2, 3, 5, 5, 8, 128),
        f32(3, 5, 5, 8, 128),
        f32(4, 16, 128),
        f32(31, 16, 128),
        f32(5, 3, 32, 128),
        f32(2, 3, 32, 128),
        f32(2, 5, 3, 8, 128),
        f32(2, 3, 32, 128),
        f32(4, 3, 8, 128),
        f32(3, 5, EXT, 128),
    ]
    return pl.pallas_call(
        kernel,
        out_shape=(pltpu.VMEM(back_temp.shape, F32), pltpu.VMEM(start_disp.shape, F32)),
        in_specs=[hbm] * 13,
        out_specs=(vmem, vmem),
        scratch_shapes=scratch
        + [
            pltpu.SemaphoreType.DMA((19,)),
            pltpu.SemaphoreType.DMA((28,)),
            pltpu.SemaphoreType.DMA((24,)),
            pltpu.SemaphoreType.DMA((1,)),
        ],
        compiler_params=pltpu.CompilerParams(collective_id=0, has_side_effects=True, vmem_limit_bytes=32 << 20),
    )(
        *(
            pltpu.with_memory_space_constraint(x, pltpu.HBM)
            for x in (
                recovery_temp, film_coeff, emissivity, char_density, back_temp, stencil_frac,
                wall_owner.reshape(1, 32), stencil_start.reshape(1, 32), live_count.reshape(1, 32),
                wall_mask, wall_dir, stiffness, start_disp,
            )
        )
    )


def solution(mesh):
    tiles = P(("gx", "gy", "gz"), None)
    flat = P(("gx", "gy", "gz"))
    in_specs = (tiles,) * 7 + (flat, flat, P("gx", "gy"), P(None, "gx", "gy"), P("gx", "gy", "gz"), P(None, "gx", "gy", "gz"))
    out_specs = (tiles, P(None, "gx", "gy", "gz"))
    return jax.shard_map(local, mesh=mesh, in_specs=in_specs, out_specs=out_specs, check_vma=False)
```
